512 devices in a mesh: space: 64 (over x, y, core), dp: 8 (over z).
Axes of the slice: x: 4, y: 8, z: 8, core: 2. Of those that a mesh axis runs over, the one named last changes fastest.
Arguments:
- features: bfloat16 [8, 16384, 128], P('dp', 'space'), may hold values from -6 to 6
- cotangent: bfloat16 [8, 16384, 128], P('dp', 'space'), may hold values from -6 to 6
- w_first: bfloat16 [27, 128, 128], replicated, may hold values from -0.109375 to 0.109375
- w_second: bfloat16 [27, 128, 128], replicated, may hold values from -0.109375 to 0.109375
- neighbors: int32 [8, 27, 16384], P('dp', None, 'space'), may hold values from 0 to 384, as said below
- send_rows: int32 [8, 64, 2, 64], P('dp', 'space'), may hold values from 0 to 255
Outputs:
- output: bfloat16 [8, 16384, 128], P('dp', 'space')
- grad_first: bfloat16 [27, 128, 128], replicated
- grad_second: bfloat16 [27, 128, 128], replicated
The draws below stay inside these ranges and needn't reach their ends.
Inputs may be any that keep to these rules, and one draw needn't show every extreme that they name: `neighbors`: offset 13 maps every voxel to its own row. Every slot row 256 .. 383 of each device's pool is referenced; the value 256 + 2 * 64 means that the neighbour is empty.
All inputs are finite; a program needn't handle non-finite values.
Results may differ from the reference program's by a relative error of at most 0.01.
Values may be sent and summed in bfloat16 or wider, within the bound.
No kernel may reach another device: no remote copies, remote signals or barrier semaphores. Data moves between devices by JAX's collectives and lax.ppermute only.
A program may use at most 64 MiB of HBM per device.

```python
import jax
import jax.numpy as jnp
from jax import lax

CHANNELS = 128
OFFSETS = 27
ROWS_DEV = 256
HALO_ROWS = 64
ROWS = 16384
N_SPACE = 64
N_DP = 8


def neighbor_block(block_key):
    slots = 2 * HALO_ROWS
    others = (OFFSETS - 1) * ROWS_DEV
    key_kind, key_local, key_remote, key_order = jax.random.split(block_key, 4)
    kinds = jax.random.randint(key_kind, (others,), 0, 10)
    local_rows = jax.random.randint(key_local, (others,), 0, ROWS_DEV)
    remote_rows = ROWS_DEV + jax.random.randint(key_remote, (others,), 0, slots)
    values = jnp.where(kinds < 6, local_rows, jnp.where(kinds < 8, remote_rows, ROWS_DEV + slots))
    order = jax.random.permutation(key_order, others)
    values = values.at[order[:slots]].set(ROWS_DEV + jnp.arange(slots))
    values = values.at[order[slots]].set(ROWS_DEV + slots)
    values = values.reshape(OFFSETS - 1, ROWS_DEV)
    center = jnp.arange(ROWS_DEV)[None, :]
    return jnp.concatenate([values[:13], center, values[13:]], 0)


def draw_neighbors(key, part):
    key = jax.random.fold_in(key, 3)
    block_keys = jax.random.split(key, N_DP * N_SPACE)
    blocks = jax.vmap(neighbor_block)(block_keys)
    blocks = blocks.reshape(N_DP, N_SPACE, OFFSETS, ROWS_DEV)
    return jnp.transpose(blocks, (0, 2, 1, 3)).reshape(N_DP, OFFSETS, N_SPACE * ROWS_DEV).astype(jnp.int32)


def draw_send_rows(key, part):
    key = jax.random.fold_in(key, 7)
    values = jax.random.randint(key, (N_DP, N_SPACE, 2, HALO_ROWS), 0, ROWS_DEV)
    values = values.at[0, 0, 0, 0].set(0)
    values = values.at[0, 0, 1, HALO_ROWS - 1].set(ROWS_DEV - 1)
    return values.astype(jnp.int32)


def block_scale(key, extent, pieces, smallest, high):
    def one(axis_at, shards_of):
        heights = jax.random.uniform(jax.random.fold_in(jax.random.fold_in(key, 6), axis_at), (shards_of,), jnp.float32, smallest / len(pieces), high / len(pieces))
        return jnp.repeat(jnp.exp(heights), extent[axis_at] // shards_of).reshape((-1,) + (1,) * (len(extent) - axis_at - 1))

    factor_of = one(*pieces[0])
    for cut in pieces[1:]:
        factor_of = factor_of * one(*cut)
    return factor_of


def gaussian(own_key, dims, spread, most, cuts=(), held_as=jnp.bfloat16):
    factor_of = block_scale(own_key, dims, cuts, -0.22, 0.18) if cuts else 1.0
    array = jax.random.normal(own_key, dims, jnp.float32) * spread * factor_of
    return jnp.minimum(jnp.maximum(array, -most), most).astype(held_as)


def setup_inputs(seed: int = 0) -> dict:
    key_list = jax.random.split(jax.random.key(seed), 7)
    return {
        "features": gaussian(key_list[0], (N_DP, ROWS, CHANNELS), 1.0, 6.0, ((0, 8), (1, 64))),
        "cotangent": gaussian(key_list[1], (N_DP, ROWS, CHANNELS), 1.0, 6.0, ((0, 8), (1, 64))),
        "w_first": gaussian(key_list[2], (OFFSETS, CHANNELS, CHANNELS), (OFFSETS * CHANNELS) ** -0.5, 0.109375),
        "w_second": gaussian(key_list[3], (OFFSETS, CHANNELS, CHANNELS), (OFFSETS * CHANNELS) ** -0.5, 0.109375),
        "neighbors": draw_neighbors(jax.random.fold_in(key_list[6], 71), 0),
        "send_rows": draw_send_rows(jax.random.fold_in(key_list[6], 71), 0),
    }


def build_pool(feat_all, device, sends):
    width = feat_all.shape[2]
    before = jnp.maximum(device - 1, 0)
    after = jnp.minimum(device + 1, N_SPACE - 1)
    zeros = jnp.zeros((HALO_ROWS, width), feat_all.dtype)
    from_before = jnp.where(device > 0, feat_all[before][sends[before, 1]], zeros)
    from_after = jnp.where(device < N_SPACE - 1, feat_all[after][sends[after, 0]], zeros)
    return jnp.concatenate([feat_all[device], from_before, from_after, jnp.zeros((1, width), feat_all.dtype)], 0)


def convolve(pooled, offset_map, weights):
    gathered = pooled[offset_map].astype(jnp.float32)
    return gathered, jnp.einsum("kvc,kcd->vd", gathered, weights.astype(jnp.float32))


def reference(features, cotangent, w_first, w_second, neighbors, send_rows):
    pool_size = ROWS_DEV + 2 * HALO_ROWS + 1
    device_ids = jnp.arange(N_SPACE, dtype=jnp.int32)

    def replica(totals, inputs):
        feats, cots, maps, sends = inputs
        feat_all = feats.reshape(N_SPACE, ROWS_DEV, CHANNELS)
        cot_all = cots.reshape(N_SPACE, ROWS_DEV, CHANNELS)
        map_all = jnp.transpose(maps.reshape(OFFSETS, N_SPACE, ROWS_DEV), (1, 0, 2))

        def first_layer(device):
            return convolve(build_pool(feat_all, device, sends), map_all[device], w_first)[1]

        pre_all = lax.map(first_layer, device_ids)
        hidden_all = jax.nn.silu(pre_all).astype(jnp.bfloat16)

        def second_layer(device):
            value = convolve(build_pool(hidden_all, device, sends), map_all[device], w_second)[1]
            return (value + feat_all[device].astype(jnp.float32)).astype(jnp.bfloat16)

        out_all = lax.map(second_layer, device_ids)

        def back_second(carry, device):
            hidden_grad, grad_two = carry
            gathered = build_pool(hidden_all, device, sends)[map_all[device]].astype(jnp.float32)
            cot_dev = cot_all[device].astype(jnp.float32)
            grad_two = grad_two + jnp.einsum("kvc,vd->kcd", gathered, cot_dev)
            contrib = jnp.einsum("vd,kcd->kvc", cot_dev, w_second.astype(jnp.float32))
            pool_grad = jax.ops.segment_sum(contrib.reshape(-1, CHANNELS), map_all[device].reshape(-1), num_segments=pool_size)
            hidden_grad = hidden_grad.at[device].add(pool_grad[:ROWS_DEV])
            before = jnp.maximum(device - 1, 0)
            after = jnp.minimum(device + 1, N_SPACE - 1)
            slots_before = jnp.where(device > 0, pool_grad[ROWS_DEV:ROWS_DEV + HALO_ROWS], 0.0)
            slots_after = jnp.where(device < N_SPACE - 1, pool_grad[ROWS_DEV + HALO_ROWS:ROWS_DEV + 2 * HALO_ROWS], 0.0)
            hidden_grad = hidden_grad.at[before, sends[before, 1]].add(slots_before)
            hidden_grad = hidden_grad.at[after, sends[after, 0]].add(slots_after)
            return (hidden_grad, grad_two), 0

        start = (jnp.zeros((N_SPACE, ROWS_DEV, CHANNELS), jnp.float32), totals[1])
        (hidden_grad, grad_two), unused = lax.scan(back_second, start, device_ids)

        def back_first(grad_one, device):
            pre_dev = pre_all[device]
            sigma = jax.nn.sigmoid(pre_dev)
            pre_grad = (hidden_grad[device] * sigma * (1.0 + pre_dev * (1.0 - sigma))).astype(jnp.bfloat16)
            gathered = build_pool(feat_all, device, sends)[map_all[device]].astype(jnp.float32)
            return grad_one + jnp.einsum("kvc,vd->kcd", gathered, pre_grad.astype(jnp.float32)), 0

        grad_one, unused_two = lax.scan(back_first, totals[0], device_ids)
        return (grad_one, grad_two), out_all.reshape(ROWS, CHANNELS)

    zero_grad = jnp.zeros((OFFSETS, CHANNELS, CHANNELS), jnp.float32)
    (grad_one, grad_two), outputs = lax.scan(replica, (zero_grad, zero_grad), (features, cotangent, neighbors, send_rows))
    return outputs, grad_one.astype(jnp.bfloat16), grad_two.astype(jnp.bfloat16)
```

```python
import jax
import jax.numpy as jnp
from jax import lax
from jax.sharding import Mesh
from jax.sharding import PartitionSpec as P

SPACE = ("x", "y", "core")
PLANE = ("y", "dp")


def extended(value, sides, width):
    for axis, dim in sides:
        size, length = (lax.axis_size(axis), value.shape[dim])
        up = [(i, (i + 1) % size) for i in range(size - 1)]
        down = [(j, i) for i, j in up]
        last = lax.slice_in_dim(value, length - width, length, axis=dim)
        initial = lax.slice_in_dim(value, 0, width, axis=dim)
        before = lax.ppermute(last, axis, up)
        after = lax.ppermute(initial, axis, down)
        value = jnp.concatenate([before, value, after], axis=dim)
    return value


def assemble(local_rows, padded, depth):
    width = local_rows.shape[1]
    return jnp.concatenate(
        [local_rows, padded[:depth], padded[3 * depth :], jnp.zeros((1, width), local_rows.dtype)],
        0,
    )


def select_rows(selector, pooled):
    return jnp.einsum("kvp,pc->kvc", selector, pooled, preferred_element_type=jnp.float32).astype(
        jnp.bfloat16
    )


def convolve(pooled, selector, weights):
    gathered = select_rows(selector, pooled)
    return (
        gathered,
        jnp.einsum("kvc,kcd->vd", gathered, weights, preferred_element_type=jnp.float32),
    )


def scattered(part, axis):
    size = lax.axis_size(axis)
    pieces = lax.all_to_all(part.reshape(size, -1, part.shape[-1]), axis, 0, 0)
    return pieces.astype(jnp.float32).sum(0).astype(jnp.bfloat16)


def collected(part, axis):
    size = lax.axis_size(axis)
    pieces = lax.all_to_all(jnp.broadcast_to(part[None], (size,) + part.shape), axis, 0, 0)
    return pieces.reshape(-1, part.shape[-1])


def summed(local_first, local_second):
    offsets, rows, width = local_first.shape
    part = jnp.concatenate([local_first, local_second], 0).astype(jnp.bfloat16).reshape(-1, width)
    part = scattered(part, "core")
    part = scattered(part, "x")
    length = part.shape[0]
    peers = lax.axis_size(PLANE)
    block = 16 * -(-length // (16 * peers))
    part = jnp.pad(part, ((0, block * peers - length), (0, 0)))
    part = collected(scattered(part, PLANE), PLANE)[:length]
    part = collected(collected(part, "x"), "core")
    part = part.reshape(2, offsets, rows, width)
    return part[0], part[1]


def per_device(features, cotangent, w_first, w_second, neighbors, send_rows):
    feats = features[0]
    cot_rows = cotangent[0]
    offset_map = neighbors[0]
    sends = send_rows[0, 0]
    flat_sends = sends.reshape(-1)
    depth = sends.shape[1]
    rows_here = feats.shape[0]
    pool_rows = rows_here + 2 * depth + 1
    selector = (
        offset_map[:, :, None] == jnp.arange(pool_rows, dtype=jnp.int32)[None, None, :]
    ).astype(jnp.bfloat16)
    send_hot = (flat_sends[:, None] == jnp.arange(rows_here, dtype=jnp.int32)[None, :]).astype(
        jnp.bfloat16
    )

    def picked(rows):
        return jnp.dot(send_hot, rows, preferred_element_type=jnp.float32).astype(jnp.bfloat16)

    padded_input = extended(picked(feats), ((SPACE, 0),), depth)
    gathered_input, pre = convolve(assemble(feats, padded_input, depth), selector, w_first)
    hidden = jax.nn.silu(pre).astype(jnp.bfloat16)
    padded_hidden = extended(picked(hidden), ((SPACE, 0),), depth)
    gathered_hidden, second = convolve(assemble(hidden, padded_hidden, depth), selector, w_second)
    output = (second + feats.astype(jnp.float32)).astype(jnp.bfloat16)
    local_second = jnp.einsum(
        "kvc,vd->kcd", gathered_hidden, cot_rows, preferred_element_type=jnp.float32
    )
    pooled_cot = jnp.einsum("kvp,vd->kpd", selector, cot_rows, preferred_element_type=jnp.float32)
    pool_grad = jnp.einsum(
        "kpd,kcd->pc", pooled_cot, w_second.astype(jnp.float32), precision=lax.Precision.HIGHEST
    )
    remote = pool_grad[rows_here : rows_here + 2 * depth]
    returned = extended(remote.astype(jnp.bfloat16), ((SPACE, 0),), depth).astype(remote.dtype)
    back_rows = jnp.concatenate([returned[:depth], returned[3 * depth :]], 0)
    hidden_grad = pool_grad[:rows_here] + jnp.dot(
        send_hot.astype(jnp.float32).T, back_rows, precision=lax.Precision.HIGHEST
    )
    sigma = jax.nn.sigmoid(pre)
    pre_grad = (hidden_grad * sigma * (1.0 + pre * (1.0 - sigma))).astype(jnp.bfloat16)
    local_first = jnp.einsum(
        "kvc,vd->kcd", gathered_input, pre_grad, preferred_element_type=jnp.float32
    )
    grad_one, grad_two = summed(local_first, local_second)
    return (output[None], grad_one, grad_two)


def solution(mesh):
    fine = Mesh(mesh.devices.reshape(4, 8, 2, 8), SPACE + ("dp",))
    placed = (
        P("dp", SPACE, None),
        P("dp", SPACE, None),
        P(),
        P(),
        P("dp", None, SPACE),
        P("dp", SPACE, None, None),
    )
    return jax.shard_map(
        per_device,
        mesh=fine,
        in_specs=placed,
        out_specs=(P("dp", SPACE, None), P(), P()),
        check_vma=False,
    )
```

```python
import jax
import jax.numpy as jnp
from jax import lax
from jax.sharding import Mesh
from jax.sharding import PartitionSpec as P

SPACE = ("x", "y", "core")
PLANE = ("x", "y")


def exchange(to_before, to_after):
    size = lax.axis_size(SPACE)
    even = [(i, i ^ 1) for i in range(size)]
    odd = [(i, ((i - 1) ^ 1) + 1) for i in range(1, size - 1)]
    first = lax.axis_index("core") == 0
    far = lax.ppermute(jnp.where(first, to_before, to_after), SPACE, odd)
    near = lax.ppermute(jnp.where(first, to_after, to_before), SPACE, even)
    return jnp.where(first, far, near), jnp.where(first, near, far)


def scattered(part, axis):
    size = lax.axis_size(axis)
    pieces = lax.all_to_all(part.reshape(size, -1, part.shape[-1]), axis, 0, 0)
    return pieces.astype(jnp.float32).sum(0).astype(jnp.bfloat16)


def collected(part, axis):
    size = lax.axis_size(axis)
    return lax.all_to_all(jnp.broadcast_to(part[None], (size,) + part.shape), axis, 0, 0)


def summed(local_first, local_second):
    offsets, rows, width = local_first.shape
    first = lax.axis_index("core") == 0
    swap = [(0, 1), (1, 0)]
    given = jnp.where(first, local_second, local_first).astype(jnp.bfloat16)
    kept = jnp.where(first, local_first, local_second)
    taken = lax.ppermute(given, "core", swap)
    part = (kept + taken.astype(jnp.float32)).astype(jnp.bfloat16).reshape(-1, width)
    length = part.shape[0]
    peers = lax.axis_size(PLANE)
    block = 16 * -(-length // (16 * peers))
    part = jnp.pad(part, ((0, block * peers - length), (0, 0)))
    part = scattered(part, PLANE)
    part = collected(part, "dp").astype(jnp.float32).sum(0).astype(jnp.bfloat16)
    part = collected(part, PLANE).reshape(-1, width)[:length].reshape(offsets, rows, width)
    other = lax.ppermute(part, "core", swap)
    return jnp.where(first, part, other), jnp.where(first, other, part)


def select_rows(selector, pooled):
    return jnp.einsum("kvp,pc->kvc", selector, pooled, preferred_element_type=jnp.float32).astype(
        jnp.bfloat16
    )


def convolve(pooled, selector, weights):
    gathered = select_rows(selector, pooled)
    return (
        gathered,
        jnp.einsum("kvc,kcd->vd", gathered, weights, preferred_element_type=jnp.float32),
    )


def per_device(features, cotangent, w_first, w_second, neighbors, send_rows):
    feats = features[0]
    cot_rows = cotangent[0]
    offset_map = neighbors[0]
    sends = send_rows[0, 0]
    flat_sends = sends.reshape(-1)
    depth = sends.shape[1]
    rows_here, width = feats.shape
    pool_rows = rows_here + 2 * depth + 1
    selector = (
        offset_map[:, :, None] == jnp.arange(pool_rows, dtype=jnp.int32)[None, None, :]
    ).astype(jnp.bfloat16)
    send_hot = (flat_sends[:, None] == jnp.arange(rows_here, dtype=jnp.int32)[None, :]).astype(
        jnp.bfloat16
    )

    def picked(rows):
        return jnp.dot(send_hot, rows, preferred_element_type=jnp.float32).astype(jnp.bfloat16)

    def assemble(rows, before, after):
        return jnp.concatenate([rows, before, after, jnp.zeros((1, width), rows.dtype)], 0)

    sent = picked(feats)
    before, after = exchange(sent[:depth], sent[depth:])
    pooled_cot = jnp.einsum("kvp,vd->kpd", selector, cot_rows, preferred_element_type=jnp.float32)
    pool_grad = jnp.einsum(
        "kpd,kcd->pc", pooled_cot, w_second.astype(jnp.float32), precision=lax.Precision.HIGHEST
    )
    remote = pool_grad[rows_here : rows_here + 2 * depth].astype(jnp.bfloat16)
    gathered_input, pre = convolve(assemble(feats, before, after), selector, w_first)
    hidden = jax.nn.silu(pre).astype(jnp.bfloat16)
    sent = picked(hidden)
    before, after = exchange(
        jnp.concatenate([sent[:depth], remote[:depth]], 0),
        jnp.concatenate([sent[depth:], remote[depth:]], 0),
    )
    gathered_hidden, second = convolve(
        assemble(hidden, before[:depth], after[:depth]), selector, w_second
    )
    output = (second + feats.astype(jnp.float32)).astype(jnp.bfloat16)
    local_second = jnp.einsum(
        "kvc,vd->kcd", gathered_hidden, cot_rows, preferred_element_type=jnp.float32
    )
    back_rows = jnp.concatenate([before[depth:], after[depth:]], 0)
    hidden_grad = pool_grad[:rows_here] + jnp.dot(
        send_hot.T, back_rows, preferred_element_type=jnp.float32
    )
    sigma = jax.nn.sigmoid(pre)
    pre_grad = (hidden_grad * sigma * (1.0 + pre * (1.0 - sigma))).astype(jnp.bfloat16)
    local_first = jnp.einsum(
        "kvc,vd->kcd", gathered_input, pre_grad, preferred_element_type=jnp.float32
    )
    grad_one, grad_two = summed(local_first, local_second)
    return (output[None], grad_one, grad_two)


def solution(mesh):
    fine = Mesh(mesh.devices.reshape(4, 8, 2, 8), SPACE + ("dp",))
    placed = (
        P("dp", SPACE, None),
        P("dp", SPACE, None),
        P(),
        P(),
        P("dp", None, SPACE),
        P("dp", SPACE, None, None),
    )
    return jax.shard_map(
        per_device,
        mesh=fine,
        in_specs=placed,
        out_specs=(P("dp", SPACE, None), P(), P()),
        check_vma=False,
    )
```

```python
import jax
import jax.numpy as jnp
from jax import lax
from jax.experimental import pallas as pl
from jax.experimental.pallas import tpu as pltpu
from jax.sharding import Mesh
from jax.sharding import PartitionSpec as P

SPACE = ("x", "y", "core")
PLANE = ("y", "dp")
BF16 = jnp.bfloat16
F32 = jnp.float32
VMEM_LIMIT = 24 * 1024 * 1024


def struct(shape, dtype):
    return jax.ShapeDtypeStruct(shape, dtype)


def run(kernel, outs, flops, *args, scratch=()):
    moved = sum(a.size * a.dtype.itemsize for a in (*args, *outs))
    return pl.pallas_call(
        kernel,
        out_shape=outs,
        in_specs=[pl.BlockSpec(memory_space=pltpu.SMEM)]
        + [pl.BlockSpec(memory_space=pltpu.VMEM)] * (len(args) - 1),
        out_specs=[pl.BlockSpec(memory_space=pltpu.VMEM)] * len(outs),
        scratch_shapes=scratch,
        compiler_params=pltpu.CompilerParams(vmem_limit_bytes=VMEM_LIMIT),
        cost_estimate=pl.CostEstimate(flops=flops, bytes_accessed=moved, transcendentals=0),
    )(*args)


def dot(left, right, over=((1,), (0,))):
    return lax.dot_general(left, right, (over, ((), ())), preferred_element_type=F32)


ROWS_BOTH = ((0,), (0,))
COLS_BOTH = ((1,), (1,))


def send_lists(core, sends_ref):
    first = core == 0
    low, high = sends_ref[0:1, :], sends_ref[1:2, :]
    return jnp.where(first, high, low), jnp.where(first, low, high)


def placed_at(rows, listed):
    return (lax.broadcasted_iota(jnp.int32, (rows, listed.shape[1]), 0) == listed).astype(BF16)


def pick_kernel(core_ref, sends_ref, feats_ref, near_ref, far_ref):
    near, far = send_lists(core_ref[0], sends_ref)
    rows = feats_ref.shape[0]
    near_ref[...] = dot(placed_at(rows, near), feats_ref[...], ROWS_BOTH).astype(BF16)
    far_ref[...] = dot(placed_at(rows, far), feats_ref[...], ROWS_BOTH).astype(BF16)


def pool_grad_kernel(core_ref, map_ref, cot_ref, weights_ref, grad_ref, columns_ref, padded):
    offsets, rows = map_ref.shape
    slots = grad_ref.shape[0]
    padded[...] = jnp.zeros_like(padded)
    padded[:offsets, :] = map_ref[...]
    columns_ref[...] = padded[...].T
    cot = cot_ref[...]
    slot = lax.broadcasted_iota(jnp.int32, (slots, rows), 0)
    total = jnp.zeros(grad_ref.shape, F32)
    for k in range(offsets):
        hot = (slot == map_ref[k : k + 1, :]).astype(BF16)
        pooled = dot(hot, cot).astype(BF16)
        total += dot(pooled, weights_ref[k], COLS_BOTH)
    grad_ref[...] = total


def fill_pool(core, pool, rows_ref, near, far):
    rows, depth = rows_ref.shape[0], near.shape[0]
    pool[:rows, :] = rows_ref[...]
    pool[pl.ds(pl.multiple_of(rows + depth * (1 - core), depth), depth), :] = near
    pool[pl.ds(pl.multiple_of(rows + depth * core, depth), depth), :] = far


def gather(columns_ref, k, pool):
    rows, slots = columns_ref.shape[0], pool.shape[0]
    slot = lax.broadcasted_iota(jnp.int32, (rows, slots), 1)
    hot = (slot == columns_ref[:, k : k + 1]).astype(BF16)
    return dot(hot, pool).astype(BF16)


def first_kernel(
    core_ref, columns_ref, feats_ref, near_ref, far_ref, weights_ref, sends_ref, grad_ref,
    gathered_ref, pre_ref, hidden_ref, to_near_ref, to_far_ref, pool,
):
    core = core_ref[0]
    rows, depth = feats_ref.shape[0], near_ref.shape[0]
    fill_pool(core, pool, feats_ref, near_ref[...], far_ref[...])
    rows_in = pool[...]
    pre = jnp.zeros(pre_ref.shape, F32)
    for k in range(weights_ref.shape[0]):
        part = gather(columns_ref, k, rows_in)
        gathered_ref[k] = part
        pre += dot(part, weights_ref[k])
    pre_ref[...] = pre
    hidden = (pre * jax.nn.sigmoid(pre)).astype(BF16)
    hidden_ref[...] = hidden
    near, far = send_lists(core, sends_ref)
    before, after = grad_ref[rows : rows + depth, :], grad_ref[rows + depth :, :]
    to_near_ref[:depth, :] = dot(placed_at(rows, near), hidden, ROWS_BOTH).astype(BF16)
    to_far_ref[:depth, :] = dot(placed_at(rows, far), hidden, ROWS_BOTH).astype(BF16)
    to_near_ref[depth:, :] = jnp.where(core == 0, after, before).astype(BF16)
    to_far_ref[depth:, :] = jnp.where(core == 0, before, after).astype(BF16)


def second_kernel(
    core_ref, columns_ref, hidden_ref, near_ref, far_ref, sends_ref, grad_ref, pre_ref, cot_ref,
    first_ref, gathered_ref, pre_grad_ref, given_ref, pool,
):
    core = core_ref[0]
    rows, depth = hidden_ref.shape[0], near_ref.shape[0] // 2
    fill_pool(core, pool, hidden_ref, near_ref[:depth, :], far_ref[:depth, :])
    near, far = send_lists(core, sends_ref)
    hidden_grad = (
        grad_ref[:rows, :]
        + dot(placed_at(rows, near), near_ref[depth:, :])
        + dot(placed_at(rows, far), far_ref[depth:, :])
    )
    pre = pre_ref[...]
    sigma = jax.nn.sigmoid(pre)
    pre_grad = (hidden_grad * sigma * (1.0 + pre * (1.0 - sigma))).astype(BF16)
    pre_grad_ref[...] = pre_grad
    rows_in = pool[...]
    for k in range(given_ref.shape[0]):
        gathered_ref[k] = gather(columns_ref, k, rows_in)

    @pl.when(core == 0)
    def _():
        cot = cot_ref[...]
        for k in range(given_ref.shape[0]):
            given_ref[k] = dot(gathered_ref[k], cot, ROWS_BOTH).astype(BF16)

    @pl.when(core != 0)
    def _():
        for k in range(given_ref.shape[0]):
            given_ref[k] = dot(first_ref[k], pre_grad, ROWS_BOTH).astype(BF16)


def third_kernel(
    core_ref, first_ref, gathered_ref, pre_grad_ref, cot_ref, feats_ref, weights_ref,
    kept_ref, output_ref,
):
    core = core_ref[0]
    offsets = kept_ref.shape[0]

    @pl.when(core == 0)
    def _():
        pre_grad = pre_grad_ref[...]
        for k in range(offsets):
            kept_ref[k] = dot(first_ref[k], pre_grad, ROWS_BOTH)

    @pl.when(core != 0)
    def _():
        cot = cot_ref[...]
        for k in range(offsets):
            kept_ref[k] = dot(gathered_ref[k], cot, ROWS_BOTH)

    total = feats_ref[...].astype(F32)
    for k in range(offsets):
        total += dot(gathered_ref[k], weights_ref[k])
    output_ref[...] = total.astype(BF16)


def exchange(near, far):
    size = lax.axis_size(SPACE)
    even = [(i, i ^ 1) for i in range(size)]
    odd = [(i, ((i - 1) ^ 1) + 1) for i in range(1, size - 1)]
    far = lax.ppermute(far, SPACE, odd)
    return lax.ppermute(near, SPACE, even), far


def scattered(part, axis):
    size = lax.axis_size(axis)
    pieces = lax.all_to_all(part.reshape(size, -1, part.shape[-1]), axis, 0, 0)
    return pieces.astype(F32).sum(0).astype(BF16)


def collected(part, axis):
    size = lax.axis_size(axis)
    pieces = lax.all_to_all(jnp.broadcast_to(part[None], (size,) + part.shape), axis, 0, 0)
    return pieces.reshape(-1, part.shape[-1])


def summed(given, finish):
    swap = [(0, 1), (1, 0)]
    taken = lax.ppermute(given, "core", swap)
    kept, output = finish()
    offsets, rows, width = kept.shape
    part = (kept + taken.astype(F32)).astype(BF16).reshape(-1, width)
    part = scattered(part, "x")
    length = part.shape[0]
    peers = lax.axis_size(PLANE)
    block = 16 * -(-length // (16 * peers))
    part = jnp.pad(part, ((0, block * peers - length), (0, 0)))
    part = collected(scattered(part, PLANE), PLANE)[:length]
    part = collected(part, "x").reshape(offsets, rows, width)
    other = lax.ppermute(part, "core", swap)
    first = lax.axis_index("core") == 0
    return output, jnp.where(first, part, other), jnp.where(first, other, part)


def per_device(features, cotangent, w_first, w_second, neighbors, send_rows):
    feats, cot, offset_map, sends = features[0], cotangent[0], neighbors[0], send_rows[0, 0]
    core = lax.axis_index("core").astype(jnp.int32).reshape(1)
    rows, width = feats.shape
    offsets = offset_map.shape[0]
    depth = sends.shape[1]
    slots = rows + 2 * depth
    hot_flops = 2 * offsets * rows * slots * width
    conv_flops = 2 * offsets * rows * width * width
    halo = struct((depth, width), BF16)
    pair = struct((2 * depth, width), BF16)
    stack = struct((offsets, rows, width), BF16)
    pool = [pltpu.VMEM((slots, width), BF16)]

    near, far = run(pick_kernel, [halo, halo], 0, core, sends, feats)
    near, far = exchange(near, far)
    pool_grad, columns = run(
        pool_grad_kernel,
        [struct((slots, width), F32), struct((rows, 128), jnp.int32)],
        hot_flops + conv_flops,
        core, offset_map, cot, w_second,
        scratch=[pltpu.VMEM((128, rows), jnp.int32)],
    )
    gathered_input, pre, hidden, near, far = run(
        first_kernel,
        [stack, struct((rows, width), F32), struct((rows, width), BF16), pair, pair],
        hot_flops + conv_flops,
        core, columns, feats, near, far, w_first, sends, pool_grad,
        scratch=pool,
    )
    near, far = exchange(near, far)
    gathered_hidden, pre_grad, given = run(
        second_kernel,
        [stack, struct((rows, width), BF16), struct((offsets, width, width), BF16)],
        hot_flops + conv_flops,
        core, columns, hidden, near, far, sends, pool_grad, pre, cot, gathered_input,
        scratch=pool,
    )

    def finish():
        return run(
            third_kernel,
            [struct((offsets, width, width), F32), struct((rows, width), BF16)],
            2 * conv_flops,
            core, gathered_input, gathered_hidden, pre_grad, cot, feats, w_second,
        )

    output, grad_one, grad_two = summed(given, finish)
    return (output[None], grad_one, grad_two)


def solution(mesh):
    fine = Mesh(mesh.devices.reshape(4, 8, 2, 8), SPACE + ("dp",))
    placed = (
        P("dp", SPACE, None),
        P("dp", SPACE, None),
        P(),
        P(),
        P("dp", None, SPACE),
        P("dp", SPACE, None, None),
    )
    return jax.shard_map(
        per_device,
        mesh=fine,
        in_specs=placed,
        out_specs=(P("dp", SPACE, None), P(), P()),
        check_vma=False,
    )
```

```python
import jax
import jax.numpy as jnp
from jax import lax
from jax.experimental import pallas as pl
from jax.experimental.pallas import tpu as pltpu
from jax.sharding import Mesh
from jax.sharding import PartitionSpec as P

SPACE = ("x", "y", "core")
PLANE = ("y", "dp")
BF16 = jnp.bfloat16
F32 = jnp.float32
VMEM_LIMIT = 24 * 1024 * 1024


def struct(shape, dtype):
    return jax.ShapeDtypeStruct(shape, dtype)


def run(kernel, outs, flops, *args, far_args=(), scratch=()):
    moved = sum(a.size * a.dtype.itemsize for a in (*args, *far_args, *outs))
    return pl.pallas_call(
        kernel,
        out_shape=outs,
        in_specs=[pl.BlockSpec(memory_space=pltpu.SMEM)]
        + [pl.BlockSpec(memory_space=pltpu.VMEM)] * (len(args) - 1)
        + [pl.BlockSpec(memory_space=pltpu.HBM)] * len(far_args),
        out_specs=[pl.BlockSpec(memory_space=pltpu.VMEM)] * len(outs),
        scratch_shapes=scratch,
        compiler_params=pltpu.CompilerParams(vmem_limit_bytes=VMEM_LIMIT),
        cost_estimate=pl.CostEstimate(flops=flops, bytes_accessed=moved, transcendentals=0),
    )(*args, *(pltpu.with_memory_space_constraint(a, pltpu.HBM) for a in far_args))


def dot(left, right, over=((1,), (0,))):
    return lax.dot_general(left, right, (over, ((), ())), preferred_element_type=F32)


ROWS_BOTH = ((0,), (0,))
COLS_BOTH = ((1,), (1,))


def send_lists(core, sends_ref):
    first = core == 0
    low, high = sends_ref[0:1, :], sends_ref[1:2, :]
    return jnp.where(first, high, low), jnp.where(first, low, high)


def placed_at(rows, listed):
    return (lax.broadcasted_iota(jnp.int32, (rows, listed.shape[1]), 0) == listed).astype(BF16)


def pick_kernel(
    core_ref, sends_hbm, feats_hbm, map_hbm, cot_hbm,
    near_ref, far_ref, sends_ref, feats_ref, map_ref, cot_ref, sems,
):
    copies = [
        pltpu.make_async_copy(source, target, sems.at[i])
        for i, (source, target) in enumerate(
            ((sends_hbm, sends_ref), (feats_hbm, feats_ref), (map_hbm, map_ref), (cot_hbm, cot_ref))
        )
    ]
    for copy in copies:
        copy.start()
    copies[0].wait()
    near, far = send_lists(core_ref[0], sends_ref)
    rows = feats_ref.shape[0]
    near, far = placed_at(rows, near), placed_at(rows, far)
    copies[1].wait()
    near_ref[...] = dot(near, feats_ref[...], ROWS_BOTH).astype(BF16)
    far_ref[...] = dot(far, feats_ref[...], ROWS_BOTH).astype(BF16)
    copies[2].wait()
    copies[3].wait()


def pool_grad_kernel(core_ref, map_ref, cot_ref, weights_hbm, grad_ref, columns_ref, padded, pooled, weights, sem):
    copy = pltpu.make_async_copy(weights_hbm, weights, sem)
    copy.start()
    offsets, rows = map_ref.shape[0], map_ref.shape[2]
    slots = grad_ref.shape[0]
    padded[...] = jnp.zeros_like(padded)
    for k in range(offsets):
        padded[k : k + 1, :] = map_ref[k]
    columns_ref[...] = padded[...].T
    cot = cot_ref[...]
    slot = lax.broadcasted_iota(jnp.int32, (slots, rows), 0)
    for k in range(offsets):
        pooled[k] = dot((slot == map_ref[k]).astype(BF16), cot).astype(BF16)
    copy.wait()
    total = jnp.zeros(grad_ref.shape, F32)
    for k in range(offsets):
        total += dot(pooled[k], weights[k], COLS_BOTH)
    grad_ref[...] = total


def fill_pool(core, pool, rows_ref, near, far):
    rows, depth = rows_ref.shape[0], near.shape[0]
    pool[:rows, :] = rows_ref[...]
    pool[pl.ds(pl.multiple_of(rows + depth * (1 - core), depth), depth), :] = near
    pool[pl.ds(pl.multiple_of(rows + depth * core, depth), depth), :] = far


def gather(columns_ref, pool_ref, gathered_ref):
    (rows, _), (slots, width) = columns_ref.shape, pool_ref.shape
    pool = pool_ref[...]
    slot = lax.broadcasted_iota(jnp.int32, (rows, slots), 1)
    for k in range(gathered_ref.shape[1] // width):
        hot = (slot == columns_ref[:, k : k + 1]).astype(BF16)
        gathered_ref[:, k * width : (k + 1) * width] = dot(hot, pool).astype(BF16)


def first_kernel(
    core_ref, columns_ref, feats_ref, near_ref, far_ref, sends_ref, grad_ref, weights_hbm,
    gathered_ref, pre_ref, hidden_ref, to_near_ref, to_far_ref, pool, weights, sem,
):
    copy = pltpu.make_async_copy(weights_hbm, weights, sem)
    copy.start()
    core = core_ref[0]
    rows, depth = feats_ref.shape[0], near_ref.shape[0]
    fill_pool(core, pool, feats_ref, near_ref[...], far_ref[...])
    gather(columns_ref, pool, gathered_ref)
    near, far = send_lists(core, sends_ref)
    before, after = grad_ref[rows : rows + depth, :], grad_ref[rows + depth :, :]
    to_near_ref[depth:, :] = jnp.where(core == 0, after, before).astype(BF16)
    to_far_ref[depth:, :] = jnp.where(core == 0, before, after).astype(BF16)
    copy.wait()
    pre = dot(gathered_ref[...], weights[...])
    pre_ref[...] = pre
    hidden = (pre * jax.nn.sigmoid(pre)).astype(BF16)
    hidden_ref[...] = hidden
    to_near_ref[:depth, :] = dot(placed_at(rows, near), hidden, ROWS_BOTH).astype(BF16)
    to_far_ref[:depth, :] = dot(placed_at(rows, far), hidden, ROWS_BOTH).astype(BF16)


def second_kernel(
    core_ref, columns_ref, hidden_ref, near_ref, far_ref, sends_ref, grad_ref, pre_ref, cot_ref,
    first_ref, gathered_ref, pre_grad_ref, given_ref, pool,
):
    core = core_ref[0]
    rows, depth = hidden_ref.shape[0], near_ref.shape[0] // 2
    fill_pool(core, pool, hidden_ref, near_ref[:depth, :], far_ref[:depth, :])
    near, far = send_lists(core, sends_ref)
    hidden_grad = (
        grad_ref[:rows, :]
        + dot(placed_at(rows, near), near_ref[depth:, :])
        + dot(placed_at(rows, far), far_ref[depth:, :])
    )
    pre = pre_ref[...]
    sigma = jax.nn.sigmoid(pre)
    pre_grad_ref[...] = (hidden_grad * sigma * (1.0 + pre * (1.0 - sigma))).astype(BF16)
    gather(columns_ref, pool, gathered_ref)

    @pl.when(core == 0)
    def _():
        given_ref[...] = dot(gathered_ref[...], cot_ref[...], ROWS_BOTH).astype(BF16)

    @pl.when(core != 0)
    def _():
        given_ref[...] = dot(first_ref[...], pre_grad_ref[...], ROWS_BOTH).astype(BF16)


def third_kernel(
    core_ref, first_ref, gathered_ref, pre_grad_ref, cot_ref, feats_ref, weights_ref,
    kept_ref, output_ref,
):
    core = core_ref[0]

    @pl.when(core == 0)
    def _():
        kept_ref[...] = dot(first_ref[...], pre_grad_ref[...], ROWS_BOTH)

    @pl.when(core != 0)
    def _():
        kept_ref[...] = dot(gathered_ref[...], cot_ref[...], ROWS_BOTH)

    output_ref[...] = (dot(gathered_ref[...], weights_ref[...]) + feats_ref[...].astype(F32)).astype(BF16)


def exchange(near, far):
    size = lax.axis_size(SPACE)
    even = [(i, i ^ 1) for i in range(size)]
    odd = [(i, ((i - 1) ^ 1) + 1) for i in range(1, size - 1)]
    far = lax.ppermute(far, SPACE, odd)
    return lax.ppermute(near, SPACE, even), far


def scattered(part, axis):
    size = lax.axis_size(axis)
    pieces = lax.all_to_all(part.reshape(size, -1, part.shape[-1]), axis, 0, 0)
    return pieces.astype(F32).sum(0).astype(BF16)


def collected(part, axis):
    size = lax.axis_size(axis)
    pieces = lax.all_to_all(jnp.broadcast_to(part[None], (size,) + part.shape), axis, 0, 0)
    return pieces.reshape(-1, part.shape[-1])


def summed(given, finish):
    swap = [(0, 1), (1, 0)]
    taken = lax.ppermute(given, "core", swap)
    kept, output = finish()
    part = (kept + taken.astype(F32)).astype(BF16)
    part = scattered(part, "x")
    length = part.shape[0]
    peers = lax.axis_size(PLANE)
    block = 16 * -(-length // (16 * peers))
    part = jnp.pad(part, ((0, block * peers - length), (0, 0)))
    part = collected(scattered(part, PLANE), PLANE)[:length]
    part = collected(part, "x")
    other = lax.ppermute(part, "core", swap)
    first = lax.axis_index("core") == 0
    return output, jnp.where(first, part, other), jnp.where(first, other, part)


def per_device(features, cotangent, w_first, w_second, neighbors, send_rows):
    core = lax.axis_index("core").astype(jnp.int32).reshape(1)
    _, rows, width = features.shape
    offsets, depth = neighbors.shape[1], send_rows.shape[-1]
    slots = rows + 2 * depth
    hot_flops = 2 * offsets * rows * slots * width
    conv_flops = 2 * offsets * rows * width * width
    own = struct((rows, width), BF16)
    halo = struct((depth, width), BF16)
    pair = struct((2 * depth, width), BF16)
    wide = struct((rows, offsets * width), BF16)
    stack = (offsets * width, width)
    sem = pltpu.SemaphoreType.DMA
    pool = pltpu.VMEM((slots, width), BF16)

    near, far, sends, feats, offset_map, cot = run(
        pick_kernel,
        [halo, halo, struct((2, depth), jnp.int32), own, struct((offsets, 1, rows), jnp.int32), own],
        0,
        core,
        far_args=(send_rows[0, 0], features[0], jnp.transpose(neighbors, (1, 0, 2)), cotangent[0]),
        scratch=[sem((4,))],
    )
    near, far = exchange(near, far)
    pool_grad, columns = run(
        pool_grad_kernel,
        [struct((slots, width), F32), struct((rows, 128), jnp.int32)],
        hot_flops + conv_flops,
        core, offset_map, cot,
        far_args=(w_second,),
        scratch=[
            pltpu.VMEM((128, rows), jnp.int32),
            pltpu.VMEM((offsets, slots, width), BF16),
            pltpu.VMEM((offsets, width, width), BF16),
            sem,
        ],
    )
    gathered_input, pre, hidden, near, far = run(
        first_kernel,
        [wide, struct((rows, width), F32), own, pair, pair],
        hot_flops + conv_flops,
        core, columns, feats, near, far, sends, pool_grad,
        far_args=(w_first.reshape(stack),),
        scratch=[pool, pltpu.VMEM(stack, BF16), sem],
    )
    near, far = exchange(near, far)
    gathered_hidden, pre_grad, given = run(
        second_kernel,
        [wide, own, struct(stack, BF16)],
        hot_flops + conv_flops,
        core, columns, hidden, near, far, sends, pool_grad, pre, cot, gathered_input,
        scratch=[pool],
    )

    def finish():
        return run(
            third_kernel,
            [struct(stack, F32), own],
            2 * conv_flops,
            core, gathered_input, gathered_hidden, pre_grad, cot, feats, w_second.reshape(stack),
        )

    output, grad_one, grad_two = summed(given, finish)
    shape = (offsets, width, width)
    return (output[None], grad_one.reshape(shape), grad_two.reshape(shape))


def solution(mesh):
    fine = Mesh(mesh.devices.reshape(4, 8, 2, 8), SPACE + ("dp",))
    placed = (
        P("dp", SPACE, None),
        P("dp", SPACE, None),
        P(),
        P(),
        P("dp", None, SPACE),
        P("dp", SPACE, None, None),
    )
    return jax.shard_map(
        per_device,
        mesh=fine,
        in_specs=placed,
        out_specs=(P("dp", SPACE, None), P(), P()),
        check_vma=False,
    )
```

```python
import jax
import jax.numpy as jnp
from jax import lax
from jax.experimental import pallas as pl
from jax.experimental.pallas import tpu as pltpu
from jax.sharding import Mesh
from jax.sharding import PartitionSpec as P

SPACE = ("x", "y", "core")
PLANE = ("y", "dp")
BF16 = jnp.bfloat16
F32 = jnp.float32
VMEM_LIMIT = 24 * 1024 * 1024


def struct(shape, dtype):
    return jax.ShapeDtypeStruct(shape, dtype)


def run(kernel, outs, flops, *args, far_args=(), scratch=()):
    moved = sum(a.size * a.dtype.itemsize for a in (*args, *far_args, *outs))
    return pl.pallas_call(
        kernel,
        out_shape=outs,
        in_specs=[pl.BlockSpec(memory_space=pltpu.SMEM)]
        + [pl.BlockSpec(memory_space=pltpu.VMEM)] * (len(args) - 1)
        + [pl.BlockSpec(memory_space=pltpu.HBM)] * len(far_args),
        out_specs=[pl.BlockSpec(memory_space=pltpu.VMEM)] * len(outs),
        scratch_shapes=scratch,
        compiler_params=pltpu.CompilerParams(vmem_limit_bytes=VMEM_LIMIT),
        cost_estimate=pl.CostEstimate(flops=flops, bytes_accessed=moved, transcendentals=0),
    )(*args, *(pltpu.with_memory_space_constraint(a, pltpu.HBM) for a in far_args))


def dot(left, right, over=((1,), (0,))):
    return lax.dot_general(left, right, (over, ((), ())), preferred_element_type=F32)


ROWS_BOTH = ((0,), (0,))
COLS_BOTH = ((1,), (1,))


def send_lists(core, sends_ref):
    first = core == 0
    low, high = sends_ref[0:1, :], sends_ref[1:2, :]
    return jnp.where(first, high, low), jnp.where(first, low, high)


def placed_at(rows, listed):
    return (lax.broadcasted_iota(jnp.int32, (rows, listed.shape[1]), 0) == listed).astype(BF16)


def pick_kernel(
    core_ref, sends_hbm, feats_hbm, map_hbm, cot_hbm, weights_hbm,
    near_ref, far_ref, sends_ref, feats_ref, map_ref, cot_ref, weights_ref, sems,
):
    pairs = (
        (sends_hbm, sends_ref),
        (feats_hbm, feats_ref),
        (map_hbm, map_ref),
        (cot_hbm, cot_ref),
        (weights_hbm, weights_ref),
    )
    copies = [pltpu.make_async_copy(*pair, sems.at[i]) for i, pair in enumerate(pairs)]
    for copy in copies:
        copy.start()
    copies[0].wait()
    near, far = send_lists(core_ref[0], sends_ref)
    rows = feats_ref.shape[0]
    near, far = placed_at(rows, near), placed_at(rows, far)
    copies[1].wait()
    near_ref[...] = dot(near, feats_ref[...], ROWS_BOTH).astype(BF16)
    far_ref[...] = dot(far, feats_ref[...], ROWS_BOTH).astype(BF16)
    for copy in copies[2:]:
        copy.wait()


def pool_grad_kernel(core_ref, map_ref, cot_ref, weights_ref, grad_ref, columns_ref, padded):
    offsets, rows = map_ref.shape[0], map_ref.shape[2]
    slots = grad_ref.shape[0]
    padded[...] = jnp.zeros_like(padded)
    for k in range(offsets):
        padded[k : k + 1, :] = map_ref[k]
    columns_ref[...] = padded[...].T
    cot = cot_ref[...]
    slot = lax.broadcasted_iota(jnp.int32, (slots, rows), 0)
    total = jnp.zeros(grad_ref.shape, F32)
    for k in range(offsets):
        pooled = dot((slot == padded[k : k + 1, :]).astype(BF16), cot).astype(BF16)
        total += dot(pooled, weights_ref[k], COLS_BOTH)
    grad_ref[...] = total


def fill_pool(core, pool, rows_ref, near, far):
    rows, depth = rows_ref.shape[0], near.shape[0]
    pool[:rows, :] = rows_ref[...]
    pool[pl.ds(pl.multiple_of(rows + depth * (1 - core), depth), depth), :] = near
    pool[pl.ds(pl.multiple_of(rows + depth * core, depth), depth), :] = far


def gather(columns_ref, pool_ref, gathered_ref):
    (rows, _), (slots, width) = columns_ref.shape, pool_ref.shape
    pool = pool_ref[...]
    slot = lax.broadcasted_iota(jnp.int32, (rows, slots), 1)
    for k in range(gathered_ref.shape[1] // width):
        hot = (slot == columns_ref[:, k : k + 1]).astype(BF16)
        gathered_ref[:, k * width : (k + 1) * width] = dot(hot, pool).astype(BF16)


def first_kernel(
    core_ref, far_ref, near_ref, columns_ref, feats_ref, sends_ref, grad_ref, weights_hbm,
    gathered_ref, pre_ref, hidden_ref, to_near_ref, to_far_ref, pool, weights, sem,
):
    copy = pltpu.make_async_copy(weights_hbm, weights, sem)
    copy.start()
    core = core_ref[0]
    rows, depth = feats_ref.shape[0], near_ref.shape[0]
    fill_pool(core, pool, feats_ref, near_ref[...], far_ref[...])
    gather(columns_ref, pool, gathered_ref)
    near, far = send_lists(core, sends_ref)
    before, after = grad_ref[rows : rows + depth, :], grad_ref[rows + depth :, :]
    to_near_ref[depth:, :] = jnp.where(core == 0, after, before).astype(BF16)
    to_far_ref[depth:, :] = jnp.where(core == 0, before, after).astype(BF16)
    copy.wait()
    pre = dot(gathered_ref[...], weights[...])
    pre_ref[...] = pre
    hidden = (pre * jax.nn.sigmoid(pre)).astype(BF16)
    hidden_ref[...] = hidden
    to_near_ref[:depth, :] = dot(placed_at(rows, near), hidden, ROWS_BOTH).astype(BF16)
    to_far_ref[:depth, :] = dot(placed_at(rows, far), hidden, ROWS_BOTH).astype(BF16)


def second_kernel(
    core_ref, far_ref, near_ref, columns_ref, hidden_ref, sends_ref, grad_ref, pre_ref, cot_ref,
    first_ref, gathered_ref, pre_grad_ref, given_ref, pool,
):
    core = core_ref[0]
    rows, depth = hidden_ref.shape[0], near_ref.shape[0] // 2
    fill_pool(core, pool, hidden_ref, near_ref[:depth, :], far_ref[:depth, :])
    near, far = send_lists(core, sends_ref)
    hidden_grad = (
        grad_ref[:rows, :]
        + dot(placed_at(rows, near), near_ref[depth:, :])
        + dot(placed_at(rows, far), far_ref[depth:, :])
    )
    pre = pre_ref[...]
    sigma = jax.nn.sigmoid(pre)
    pre_grad_ref[...] = (hidden_grad * sigma * (1.0 + pre * (1.0 - sigma))).astype(BF16)
    gather(columns_ref, pool, gathered_ref)

    @pl.when(core == 0)
    def _():
        given_ref[...] = dot(gathered_ref[...], cot_ref[...], ROWS_BOTH).astype(BF16)

    @pl.when(core != 0)
    def _():
        given_ref[...] = dot(first_ref[...], pre_grad_ref[...], ROWS_BOTH).astype(BF16)


def third_kernel(
    core_ref, first_ref, gathered_ref, pre_grad_ref, cot_ref, feats_ref, weights_ref,
    kept_ref, output_ref,
):
    core = core_ref[0]

    @pl.when(core == 0)
    def _():
        kept_ref[...] = dot(first_ref[...], pre_grad_ref[...], ROWS_BOTH)

    @pl.when(core != 0)
    def _():
        kept_ref[...] = dot(gathered_ref[...], cot_ref[...], ROWS_BOTH)

    output_ref[...] = (dot(gathered_ref[...], weights_ref[...]) + feats_ref[...].astype(F32)).astype(BF16)


def exchange(near, far):
    size = lax.axis_size(SPACE)
    even = [(i, i ^ 1) for i in range(size)]
    odd = [(i, ((i - 1) ^ 1) + 1) for i in range(1, size - 1)]
    far = lax.ppermute(far, SPACE, odd)
    return lax.ppermute(near, SPACE, even), far


def scattered(part, axis):
    size = lax.axis_size(axis)
    pieces = lax.all_to_all(part.reshape(size, -1, part.shape[-1]), axis, 0, 0)
    return pieces.astype(F32).sum(0).astype(BF16)


def collected(part, axis):
    size = lax.axis_size(axis)
    pieces = lax.all_to_all(jnp.broadcast_to(part[None], (size,) + part.shape), axis, 0, 0)
    return pieces.reshape(-1, part.shape[-1])


def summed(given, finish):
    swap = [(0, 1), (1, 0)]
    taken = lax.ppermute(given, "core", swap)
    kept, output = finish()
    part = (kept + taken.astype(F32)).astype(BF16)
    part = scattered(part, "x")
    length = part.shape[0]
    peers = lax.axis_size(PLANE)
    block = 16 * -(-length // (16 * peers))
    part = jnp.pad(part, ((0, block * peers - length), (0, 0)))
    part = collected(scattered(part, PLANE), PLANE)[:length]
    part = collected(part, "x")
    other = lax.ppermute(part, "core", swap)
    first = lax.axis_index("core") == 0
    return output, jnp.where(first, part, other), jnp.where(first, other, part)


def per_device(features, cotangent, w_first, w_second, neighbors, send_rows):
    core = lax.axis_index("core").astype(jnp.int32).reshape(1)
    _, rows, width = features.shape
    offsets, depth = neighbors.shape[1], send_rows.shape[-1]
    slots = rows + 2 * depth
    hot_flops = 2 * offsets * rows * slots * width
    conv_flops = 2 * offsets * rows * width * width
    own = struct((rows, width), BF16)
    halo = struct((depth, width), BF16)
    pair = struct((2 * depth, width), BF16)
    wide = struct((rows, offsets * width), BF16)
    stack = (offsets * width, width)
    sem = pltpu.SemaphoreType.DMA
    pool = pltpu.VMEM((slots, width), BF16)

    near, far, sends, feats, offset_map, cot, weights = run(
        pick_kernel,
        [
            halo, halo, struct((2, depth), jnp.int32), own,
            struct((offsets, 1, rows), jnp.int32), own, struct(w_second.shape, BF16),
        ],
        0,
        core,
        far_args=(
            send_rows[0, 0], features[0], jnp.transpose(neighbors, (1, 0, 2)), cotangent[0], w_second,
        ),
        scratch=[sem((5,))],
    )
    near, far = exchange(near, far)
    pool_grad, columns = run(
        pool_grad_kernel,
        [struct((slots, width), F32), struct((rows, 128), jnp.int32)],
        hot_flops + conv_flops,
        core, offset_map, cot, weights,
        scratch=[pltpu.VMEM((128, rows), jnp.int32)],
    )
    gathered_input, pre, hidden, near, far = run(
        first_kernel,
        [wide, struct((rows, width), F32), own, pair, pair],
        hot_flops + conv_flops,
        core, far, near, columns, feats, sends, pool_grad,
        far_args=(w_first.reshape(stack),),
        scratch=[pool, pltpu.VMEM(stack, BF16), sem],
    )
    near, far = exchange(near, far)
    gathered_hidden, pre_grad, given = run(
        second_kernel,
        [wide, own, struct(stack, BF16)],
        hot_flops + conv_flops,
        core, far, near, columns, hidden, sends, pool_grad, pre, cot, gathered_input,
        scratch=[pool],
    )

    def finish():
        return run(
            third_kernel,
            [struct(stack, F32), own],
            2 * conv_flops,
            core, gathered_input, gathered_hidden, pre_grad, cot, feats, weights.reshape(stack),
        )

    output, grad_one, grad_two = summed(given, finish)
    shape = (offsets, width, width)
    return (output[None], grad_one.reshape(shape), grad_two.reshape(shape))


def solution(mesh):
    fine = Mesh(mesh.devices.reshape(4, 8, 2, 8), SPACE + ("dp",))
    placed = (
        P("dp", SPACE, None),
        P("dp", SPACE, None),
        P(),
        P(),
        P("dp", None, SPACE),
        P("dp", SPACE, None, None),
    )
    return jax.shard_map(
        per_device,
        mesh=fine,
        in_specs=placed,
        out_specs=(P("dp", SPACE, None), P(), P()),
        check_vma=False,
    )
```

```python
import jax
import jax.numpy as jnp
from jax import lax
from jax.experimental import pallas as pl
from jax.experimental.pallas import tpu as pltpu
from jax.sharding import Mesh
from jax.sharding import PartitionSpec as P

SPACE = ("x", "y", "core")
PLANE = ("y", "dp")
BF16 = jnp.bfloat16
F32 = jnp.float32
VMEM_LIMIT = 24 * 1024 * 1024


def struct(shape, dtype):
    return jax.ShapeDtypeStruct(shape, dtype)


def run(kernel, outs, flops, *args, far_args=(), any_args=(), scratch=()):
    moved = sum(a.size * a.dtype.itemsize for a in (*args, *far_args, *outs))
    return pl.pallas_call(
        kernel,
        out_shape=outs,
        in_specs=[pl.BlockSpec(memory_space=pltpu.SMEM)]
        + [pl.BlockSpec(memory_space=pltpu.VMEM)] * (len(args) - 1)
        + [pl.BlockSpec(memory_space=pltpu.HBM)] * len(far_args)
        + [pl.BlockSpec(memory_space=pl.ANY)] * len(any_args),
        out_specs=[pl.BlockSpec(memory_space=pltpu.VMEM)] * len(outs),
        scratch_shapes=scratch,
        compiler_params=pltpu.CompilerParams(vmem_limit_bytes=VMEM_LIMIT),
        cost_estimate=pl.CostEstimate(flops=flops, bytes_accessed=moved, transcendentals=0),
    )(*args, *(pltpu.with_memory_space_constraint(a, pltpu.HBM) for a in far_args), *any_args)


def dot(left, right, over=((1,), (0,))):
    return lax.dot_general(left, right, (over, ((), ())), preferred_element_type=F32)


ROWS_BOTH = ((0,), (0,))
COLS_BOTH = ((1,), (1,))


def send_lists(core, sends_ref):
    first = core == 0
    low, high = sends_ref[0:1, :], sends_ref[1:2, :]
    return jnp.where(first, high, low), jnp.where(first, low, high)


def placed_at(rows, listed):
    return (lax.broadcasted_iota(jnp.int32, (rows, listed.shape[1]), 0) == listed).astype(BF16)


def pick_kernel(
    core_ref, sends_hbm, feats_hbm, map_hbm, cot_hbm, weights_hbm,
    near_ref, far_ref, sends_ref, feats_ref, map_ref, cot_ref, weights_ref, sems,
):
    pairs = (
        (sends_hbm, sends_ref),
        (feats_hbm, feats_ref),
        (map_hbm, map_ref),
        (cot_hbm, cot_ref),
        (weights_hbm, weights_ref),
    )
    copies = [pltpu.make_async_copy(*pair, sems.at[i]) for i, pair in enumerate(pairs)]
    for copy in copies:
        copy.start()
    copies[0].wait()
    near, far = send_lists(core_ref[0], sends_ref)
    rows = feats_ref.shape[0]
    near, far = placed_at(rows, near), placed_at(rows, far)
    copies[1].wait()
    near_ref[...] = dot(near, feats_ref[...], ROWS_BOTH).astype(BF16)
    far_ref[...] = dot(far, feats_ref[...], ROWS_BOTH).astype(BF16)
    for copy in copies[2:]:
        copy.wait()


def pool_slots(rows_ref, cot_ref, weights_ref, first_slot, grad_ref, pooled_ref):
    slots, width = grad_ref.shape
    rows = rows_ref.shape[1]
    cot = cot_ref[...]
    slot = lax.broadcasted_iota(jnp.int32, (slots, rows), 0) + first_slot
    total = jnp.zeros(grad_ref.shape, F32)
    for k in range(weights_ref.shape[0]):
        pooled = dot((slot == rows_ref[k : k + 1, :]).astype(BF16), cot).astype(BF16)
        pooled_ref[:, k * width : (k + 1) * width] = pooled
        total += dot(pooled, weights_ref[k], COLS_BOTH)
    grad_ref[...] = total


def copied_slots_kernel(core_ref, map_ref, cot_ref, weights_ref, grad_ref, pooled_ref, columns_ref, rows_ref):
    rows_ref[...] = jnp.zeros_like(rows_ref)
    for k in range(map_ref.shape[0]):
        rows_ref[k : k + 1, :] = map_ref[k]
    columns_ref[...] = rows_ref[...].T
    pool_slots(rows_ref, cot_ref, weights_ref, cot_ref.shape[0], grad_ref, pooled_ref)


def own_slots_kernel(core_ref, rows_ref, cot_ref, weights_ref, hidden_ref, grad_ref, pooled_ref):
    pool_slots(rows_ref, cot_ref, weights_ref, 0, grad_ref, pooled_ref)


def fill_pool(core, pool, rows_ref, near, far):
    rows, depth = rows_ref.shape[0], near.shape[0]
    pool[:rows, :] = rows_ref[...]
    pool[pl.ds(pl.multiple_of(rows + depth * (1 - core), depth), depth), :] = near
    pool[pl.ds(pl.multiple_of(rows + depth * core, depth), depth), :] = far


def gather(columns_ref, pool_ref, gathered_ref):
    (rows, _), (slots, width) = columns_ref.shape, pool_ref.shape
    pool = pool_ref[...]
    slot = lax.broadcasted_iota(jnp.int32, (rows, slots), 1)
    for k in range(gathered_ref.shape[1] // width):
        hot = (slot == columns_ref[:, k : k + 1]).astype(BF16)
        gathered_ref[:, k * width : (k + 1) * width] = dot(hot, pool).astype(BF16)


def first_kernel(
    core_ref, far_ref, near_ref, columns_ref, feats_ref, sends_ref, grad_ref, weights_hbm,
    gathered_ref, pre_ref, hidden_ref, to_near_ref, to_far_ref, pool, weights, sem,
):
    copy = pltpu.make_async_copy(weights_hbm, weights, sem)
    copy.start()
    core = core_ref[0]
    rows, depth = feats_ref.shape[0], near_ref.shape[0]
    fill_pool(core, pool, feats_ref, near_ref[...], far_ref[...])
    gather(columns_ref, pool, gathered_ref)
    near, far = send_lists(core, sends_ref)
    before, after = grad_ref[:depth, :], grad_ref[depth:, :]
    to_near_ref[depth:, :] = jnp.where(core == 0, after, before).astype(BF16)
    to_far_ref[depth:, :] = jnp.where(core == 0, before, after).astype(BF16)
    copy.wait()
    pre = dot(gathered_ref[...], weights[...])
    pre_ref[...] = pre
    hidden = (pre * jax.nn.sigmoid(pre)).astype(BF16)
    hidden_ref[...] = hidden
    to_near_ref[:depth, :] = dot(placed_at(rows, near), hidden, ROWS_BOTH).astype(BF16)
    to_far_ref[:depth, :] = dot(placed_at(rows, far), hidden, ROWS_BOTH).astype(BF16)


def first_gradient(gathered_ref, pre_grad_ref, out_ref):
    out_ref[...] = dot(gathered_ref[...], pre_grad_ref[...], ROWS_BOTH).astype(out_ref.dtype)


def second_gradient(pool_ref, own_ref, copied_ref, out_ref):
    rows, wide = own_ref.shape
    width = pool_ref.shape[1]
    own, copied = pool_ref[:rows, :], pool_ref[rows:, :]
    for start in range(0, wide, 2 * width):
        stop = min(wide, start + 2 * width)
        part = dot(own, own_ref[:, start:stop], ROWS_BOTH) + dot(copied, copied_ref[:, start:stop], ROWS_BOTH)
        for column in range(start, stop, width):
            out_ref[column : column + width, :] = part[:, column - start : column - start + width].astype(
                out_ref.dtype
            )


def second_kernel(
    core_ref, far_ref, near_ref, hidden_ref, sends_ref, grad_ref, pre_ref, first_ref, own_ref, copied_ref,
    pre_grad_ref, given_ref, pool_ref,
):
    core = core_ref[0]
    rows, depth = hidden_ref.shape[0], near_ref.shape[0] // 2
    fill_pool(core, pool_ref, hidden_ref, near_ref[:depth, :], far_ref[:depth, :])
    near, far = send_lists(core, sends_ref)
    hidden_grad = (
        grad_ref[...]
        + dot(placed_at(rows, near), near_ref[depth:, :])
        + dot(placed_at(rows, far), far_ref[depth:, :])
    )
    pre = pre_ref[...]
    sigma = jax.nn.sigmoid(pre)
    pre_grad_ref[...] = (hidden_grad * sigma * (1.0 + pre * (1.0 - sigma))).astype(BF16)

    @pl.when(core == 0)
    def _():
        second_gradient(pool_ref, own_ref, copied_ref, given_ref)

    @pl.when(core != 0)
    def _():
        first_gradient(first_ref, pre_grad_ref, given_ref)


def third_kernel(core_ref, first_ref, pre_grad_ref, pool_ref, own_ref, copied_ref, kept_ref):
    core = core_ref[0]

    @pl.when(core == 0)
    def _():
        first_gradient(first_ref, pre_grad_ref, kept_ref)

    @pl.when(core != 0)
    def _():
        second_gradient(pool_ref, own_ref, copied_ref, kept_ref)


def output_kernel(core_ref, columns_ref, pool_ref, feats_ref, weights_ref, summed_ref, output_ref, gathered):
    gather(columns_ref, pool_ref, gathered)
    output_ref[...] = (dot(gathered[...], weights_ref[...]) + feats_ref[...].astype(F32)).astype(BF16)


def exchange(near, far):
    size = lax.axis_size(SPACE)
    even = [(i, i ^ 1) for i in range(size)]
    odd = [(i, ((i - 1) ^ 1) + 1) for i in range(1, size - 1)]
    far = lax.ppermute(far, SPACE, odd)
    return lax.ppermute(near, SPACE, even), far


def scattered(part, axis):
    size = lax.axis_size(axis)
    pieces = lax.all_to_all(part.reshape(size, -1, part.shape[-1]), axis, 0, 0)
    return pieces.astype(F32).sum(0).astype(BF16)


def collected(part, axis):
    size = lax.axis_size(axis)
    pieces = lax.all_to_all(jnp.broadcast_to(part[None], (size,) + part.shape), axis, 0, 0)
    return pieces.reshape(-1, part.shape[-1])


def summed(given, keep, beside):
    swap = [(0, 1), (1, 0)]
    taken = lax.ppermute(given, "core", swap)
    part = (keep() + taken.astype(F32)).astype(BF16)
    part = scattered(part, "x")
    length = part.shape[0]
    peers = lax.axis_size(PLANE)
    block = 16 * -(-length // (16 * peers))
    part = jnp.pad(part, ((0, block * peers - length), (0, 0)))
    part = collected(scattered(part, PLANE), PLANE)[:length]
    part = collected(part, "x")
    other = lax.ppermute(part, "core", swap)
    output = beside(part)
    first = lax.axis_index("core") == 0
    return output, jnp.where(first, part, other), jnp.where(first, other, part)


def per_device(features, cotangent, w_first, w_second, neighbors, send_rows):
    core = lax.axis_index("core").astype(jnp.int32).reshape(1)
    _, rows, width = features.shape
    offsets, depth = neighbors.shape[1], send_rows.shape[-1]
    copied, slots = 2 * depth, rows + 2 * depth
    hot_flops = 2 * offsets * rows * slots * width
    conv_flops = 2 * offsets * rows * width * width
    own = struct((rows, width), BF16)
    halo = struct((depth, width), BF16)
    pair = struct((2 * depth, width), BF16)
    wide = struct((rows, offsets * width), BF16)
    stack = (offsets * width, width)
    sem = pltpu.SemaphoreType.DMA
    pool = struct((slots, width), BF16)

    near, far, sends, feats, offset_map, cot, weights = run(
        pick_kernel,
        [
            halo, halo, struct((2, depth), jnp.int32), own,
            struct((offsets, 1, rows), jnp.int32), own, struct(w_second.shape, BF16),
        ],
        0,
        core,
        far_args=(
            send_rows[0, 0], features[0], jnp.transpose(neighbors, (1, 0, 2)), cotangent[0], w_second,
        ),
        scratch=[sem((5,))],
    )
    near, far = exchange(near, far)
    copied_grad, copied_pooled, columns, map_rows = run(
        copied_slots_kernel,
        [
            struct((copied, width), F32), struct((copied, offsets * width), BF16),
            struct((rows, 128), jnp.int32), struct((128, rows), jnp.int32),
        ],
        hot_flops // 3,
        core, offset_map, cot, weights,
    )
    gathered_input, pre, hidden, near, far = run(
        first_kernel,
        [wide, struct((rows, width), F32), own, pair, pair],
        hot_flops + conv_flops,
        core, far, near, columns, feats, sends, copied_grad,
        far_args=(w_first.reshape(stack),),
        scratch=[pltpu.VMEM(pool.shape, BF16), pltpu.VMEM(stack, BF16), sem],
    )
    near, far = exchange(near, far)
    own_grad, own_pooled = run(
        own_slots_kernel,
        [struct((rows, width), F32), wide],
        hot_flops,
        core, map_rows, cot, weights, hidden,
    )
    pre_grad, given, hidden_pool = run(
        second_kernel,
        [own, struct(stack, BF16), pool],
        conv_flops,
        core, far, near, hidden, sends, own_grad, pre, gathered_input, own_pooled, copied_pooled,
    )

    def keep():
        return run(
            third_kernel,
            [struct(stack, F32)],
            conv_flops,
            core, gathered_input, pre_grad, hidden_pool, own_pooled, copied_pooled,
        )[0]

    def beside(part):
        return run(
            output_kernel,
            [own],
            hot_flops + conv_flops,
            core, columns, hidden_pool, feats, weights.reshape(stack),
            any_args=(part,),
            scratch=[pltpu.VMEM(wide.shape, BF16)],
        )[0]

    output, grad_one, grad_two = summed(given, keep, beside)
    shape = (offsets, width, width)
    return (output[None], grad_one.reshape(shape), grad_two.reshape(shape))


def solution(mesh):
    fine = Mesh(mesh.devices.reshape(4, 8, 2, 8), SPACE + ("dp",))
    placed = (
        P("dp", SPACE, None),
        P("dp", SPACE, None),
        P(),
        P(),
        P("dp", None, SPACE),
        P("dp", SPACE, None, None),
    )
    return jax.shard_map(
        per_device,
        mesh=fine,
        in_specs=placed,
        out_specs=(P("dp", SPACE, None), P(), P()),
        check_vma=False,
    )
```

```python
import jax
import jax.numpy as jnp
from jax import lax
from jax.experimental import pallas as pl
from jax.experimental.pallas import tpu as pltpu
from jax.sharding import Mesh
from jax.sharding import PartitionSpec as P

SPACE = ("x", "y", "core")
PLANE = ("y", "dp")
BF16 = jnp.bfloat16
F32 = jnp.float32
VMEM_LIMIT = 24 * 1024 * 1024


def struct(shape, dtype):
    return jax.ShapeDtypeStruct(shape, dtype)


def run(kernel, outs, flops, *args, far_args=(), any_args=(), scratch=(), out_spaces=None, aliases=()):
    moved = sum(a.size * a.dtype.itemsize for a in (*args, *far_args, *outs))
    return pl.pallas_call(
        kernel,
        out_shape=outs,
        in_specs=[pl.BlockSpec(memory_space=pltpu.SMEM)]
        + [pl.BlockSpec(memory_space=pltpu.VMEM)] * (len(args) - 1)
        + [pl.BlockSpec(memory_space=pltpu.HBM)] * len(far_args)
        + [pl.BlockSpec(memory_space=pl.ANY)] * len(any_args),
        out_specs=[pl.BlockSpec(memory_space=space) for space in out_spaces or [pltpu.VMEM] * len(outs)],
        scratch_shapes=scratch,
        input_output_aliases=dict(aliases),
        compiler_params=pltpu.CompilerParams(vmem_limit_bytes=VMEM_LIMIT),
        cost_estimate=pl.CostEstimate(flops=flops, bytes_accessed=moved, transcendentals=0),
    )(*args, *(pltpu.with_memory_space_constraint(a, pltpu.HBM) for a in far_args), *any_args)


def dot(left, right, over=((1,), (0,))):
    return lax.dot_general(left, right, (over, ((), ())), preferred_element_type=F32)


ROWS_BOTH = ((0,), (0,))
COLS_BOTH = ((1,), (1,))


def send_lists(core, sends_ref):
    first = core == 0
    low, high = sends_ref[0:1, :], sends_ref[1:2, :]
    return jnp.where(first, high, low), jnp.where(first, low, high)


def placed_at(rows, listed):
    return (lax.broadcasted_iota(jnp.int32, (rows, listed.shape[1]), 0) == listed).astype(BF16)


def pick_kernel(
    core_ref, sends_hbm, feats_hbm, map_hbm, cot_hbm, weights_hbm,
    near_ref, far_ref, sends_ref, feats_ref, map_ref, cot_ref, weights_ref, sems,
):
    pairs = (
        (sends_hbm, sends_ref),
        (feats_hbm, feats_ref),
        (map_hbm, map_ref),
        (cot_hbm, cot_ref),
        (weights_hbm, weights_ref),
    )
    copies = [pltpu.make_async_copy(*pair, sems.at[i]) for i, pair in enumerate(pairs)]
    for copy in copies:
        copy.start()
    copies[0].wait()
    near, far = send_lists(core_ref[0], sends_ref)
    rows = feats_ref.shape[0]
    near, far = placed_at(rows, near), placed_at(rows, far)
    copies[1].wait()
    near_ref[...] = dot(near, feats_ref[...], ROWS_BOTH).astype(BF16)
    far_ref[...] = dot(far, feats_ref[...], ROWS_BOTH).astype(BF16)
    for copy in copies[2:]:
        copy.wait()


def pool_slots(rows_ref, cot_ref, first_slot, pooled_ref, width):
    slots, rows = pooled_ref.shape[0], rows_ref.shape[1]
    cot = cot_ref[...]
    slot = lax.broadcasted_iota(jnp.int32, (slots, rows), 0) + first_slot
    for k in range(pooled_ref.shape[1] // width):
        hot = (slot == rows_ref[k : k + 1, :]).astype(BF16)
        pooled_ref[:, k * width : (k + 1) * width] = dot(hot, cot).astype(BF16)


def copied_slots_kernel(core_ref, map_ref, cot_ref, weights_ref, grad_ref, pooled_ref, columns_ref, rows_ref):
    rows_ref[...] = jnp.zeros_like(rows_ref)
    offsets, width, _ = weights_ref.shape
    for k in range(offsets):
        rows_ref[k : k + 1, :] = map_ref[k]
    columns_ref[...] = rows_ref[...].T
    pool_slots(rows_ref, cot_ref, cot_ref.shape[0], pooled_ref, width)
    total = jnp.zeros(grad_ref.shape, F32)
    for k in range(offsets):
        total += dot(pooled_ref[:, k * width : (k + 1) * width], weights_ref[k], COLS_BOTH)
    grad_ref[...] = total


def own_slots_kernel(core_ref, rows_ref, cot_ref, weights_ref, hidden_ref, grad_ref, pooled_ref):
    pool_slots(rows_ref, cot_ref, 0, pooled_ref, cot_ref.shape[1])
    grad_ref[...] = dot(pooled_ref[...], weights_ref[...], COLS_BOTH)


def fill_pool(core, pool, rows_ref, near, far):
    rows, depth = rows_ref.shape[0], near.shape[0]
    pool[:rows, :] = rows_ref[...]
    pool[pl.ds(pl.multiple_of(rows + depth * (1 - core), depth), depth), :] = near
    pool[pl.ds(pl.multiple_of(rows + depth * core, depth), depth), :] = far


def gather(columns_ref, pool_ref, gathered_ref):
    (rows, _), (slots, width) = columns_ref.shape, pool_ref.shape
    pool = pool_ref[...]
    slot = lax.broadcasted_iota(jnp.int32, (rows, slots), 1)
    for k in range(gathered_ref.shape[1] // width):
        hot = (slot == columns_ref[:, k : k + 1]).astype(BF16)
        gathered_ref[:, k * width : (k + 1) * width] = dot(hot, pool).astype(BF16)


def first_kernel(
    core_ref, far_ref, near_ref, columns_ref, feats_ref, sends_ref, grad_ref, weights_hbm, second_hbm,
    gathered_ref, pre_ref, hidden_ref, to_near_ref, to_far_ref, second_ref, pool, weights, sem, sems,
):
    copy = pltpu.make_async_copy(weights_hbm, weights, sem)
    copy.start()
    width = weights.shape[1]
    others = [
        pltpu.make_async_copy(second_hbm.at[k], second_ref.at[:, pl.ds(k * width, width)], sems.at[k])
        for k in range(second_hbm.shape[0])
    ]
    for other in others:
        other.start()
    core = core_ref[0]
    rows, depth = feats_ref.shape[0], near_ref.shape[0]
    fill_pool(core, pool, feats_ref, near_ref[...], far_ref[...])
    gather(columns_ref, pool, gathered_ref)
    near, far = send_lists(core, sends_ref)
    before, after = grad_ref[:depth, :], grad_ref[depth:, :]
    to_near_ref[depth:, :] = jnp.where(core == 0, after, before).astype(BF16)
    to_far_ref[depth:, :] = jnp.where(core == 0, before, after).astype(BF16)
    copy.wait()
    pre = dot(gathered_ref[...], weights[...])
    pre_ref[...] = pre
    hidden = (pre * jax.nn.sigmoid(pre)).astype(BF16)
    hidden_ref[...] = hidden
    to_near_ref[:depth, :] = dot(placed_at(rows, near), hidden, ROWS_BOTH).astype(BF16)
    to_far_ref[:depth, :] = dot(placed_at(rows, far), hidden, ROWS_BOTH).astype(BF16)
    for other in others:
        other.wait()


def first_gradient(gathered_ref, pre_grad_ref, out_ref):
    out_ref[...] = dot(gathered_ref[...], pre_grad_ref[...], ROWS_BOTH).astype(out_ref.dtype)


def second_gradient(pool_ref, own_ref, copied_ref, out_ref):
    rows, wide = own_ref.shape
    width = pool_ref.shape[1]
    own, copied = pool_ref[:rows, :], pool_ref[rows:, :]
    for start in range(0, wide, 2 * width):
        stop = min(wide, start + 2 * width)
        part = dot(own, own_ref[:, start:stop], ROWS_BOTH) + dot(copied, copied_ref[:, start:stop], ROWS_BOTH)
        for column in range(start, stop, width):
            out_ref[column : column + width, :] = part[:, column - start : column - start + width].astype(
                out_ref.dtype
            )


def second_kernel(
    core_ref, far_ref, near_ref, hidden_ref, sends_ref, grad_ref, pre_ref, first_ref, own_ref, copied_ref,
    pre_grad_ref, given_ref, pool_ref,
):
    core = core_ref[0]
    rows, depth = hidden_ref.shape[0], near_ref.shape[0] // 2
    fill_pool(core, pool_ref, hidden_ref, near_ref[:depth, :], far_ref[:depth, :])
    near, far = send_lists(core, sends_ref)
    hidden_grad = (
        grad_ref[...]
        + dot(placed_at(rows, near), near_ref[depth:, :])
        + dot(placed_at(rows, far), far_ref[depth:, :])
    )
    pre = pre_ref[...]
    sigma = jax.nn.sigmoid(pre)
    pre_grad_ref[...] = (hidden_grad * sigma * (1.0 + pre * (1.0 - sigma))).astype(BF16)

    @pl.when(core == 0)
    def _():
        second_gradient(pool_ref, own_ref, copied_ref, given_ref)

    @pl.when(core != 0)
    def _():
        first_gradient(first_ref, pre_grad_ref, given_ref)


def third_kernel(
    core_ref, first_ref, pre_grad_ref, pool_ref, own_ref, copied_ref, columns_ref, kept_ref, gathered_ref
):
    core = core_ref[0]
    gather(columns_ref, pool_ref, gathered_ref)

    @pl.when(core == 0)
    def _():
        first_gradient(first_ref, pre_grad_ref, kept_ref)

    @pl.when(core != 0)
    def _():
        second_gradient(pool_ref, own_ref, copied_ref, kept_ref)


def output_kernel(
    core_ref, gathered_ref, feats_ref, weights_ref, part_any, output_ref, one_hbm, two_hbm, sems
):
    first = core_ref[0] == 0
    to_one = pltpu.make_async_copy(part_any, one_hbm, sems.at[0])
    to_two = pltpu.make_async_copy(part_any, two_hbm, sems.at[1])
    pl.when(first)(to_one.start)
    pl.when(jnp.logical_not(first))(to_two.start)
    output_ref[...] = (dot(gathered_ref[...], weights_ref[...]) + feats_ref[...].astype(F32)).astype(BF16)
    pl.when(first)(to_one.wait)
    pl.when(jnp.logical_not(first))(to_two.wait)


def last_kernel(core_ref, other_any, one_in, two_in, one_hbm, two_hbm, sems):
    first = core_ref[0] == 0
    to_one = pltpu.make_async_copy(other_any, one_hbm, sems.at[0])
    to_two = pltpu.make_async_copy(other_any, two_hbm, sems.at[1])
    pl.when(first)(to_two.start)
    pl.when(jnp.logical_not(first))(to_one.start)
    pl.when(first)(to_two.wait)
    pl.when(jnp.logical_not(first))(to_one.wait)


def exchange(near, far):
    size = lax.axis_size(SPACE)
    even = [(i, i ^ 1) for i in range(size)]
    odd = [(i, ((i - 1) ^ 1) + 1) for i in range(1, size - 1)]
    far = lax.ppermute(far, SPACE, odd)
    return lax.ppermute(near, SPACE, even), far


def scattered(part, axis):
    size = lax.axis_size(axis)
    pieces = lax.all_to_all(part.reshape(size, -1, part.shape[-1]), axis, 0, 0)
    return pieces.astype(F32).sum(0).astype(BF16)


def collected(part, axis):
    size = lax.axis_size(axis)
    pieces = lax.all_to_all(jnp.broadcast_to(part[None], (size,) + part.shape), axis, 0, 0)
    return pieces.reshape(-1, part.shape[-1])


def summed(given, keep, beside):
    swap = [(0, 1), (1, 0)]
    taken = lax.ppermute(given, "core", swap)
    part = (keep() + taken.astype(F32)).astype(BF16)
    part = scattered(part, "x")
    length = part.shape[0]
    peers = lax.axis_size(PLANE)
    block = 16 * -(-length // (16 * peers))
    part = jnp.pad(part, ((0, block * peers - length), (0, 0)))
    part = collected(scattered(part, PLANE), PLANE)[:length]
    part = collected(part, "x")
    other = lax.ppermute(part, "core", swap)
    return beside(part), other


def per_device(features, cotangent, w_first, w_second, neighbors, send_rows):
    core = lax.axis_index("core").astype(jnp.int32).reshape(1)
    _, rows, width = features.shape
    offsets, depth = neighbors.shape[1], send_rows.shape[-1]
    copied, slots = 2 * depth, rows + 2 * depth
    hot_flops = 2 * offsets * rows * slots * width
    conv_flops = 2 * offsets * rows * width * width
    own = struct((rows, width), BF16)
    halo = struct((depth, width), BF16)
    pair = struct((2 * depth, width), BF16)
    wide = struct((rows, offsets * width), BF16)
    stack = (offsets * width, width)
    sem = pltpu.SemaphoreType.DMA
    pool = struct((slots, width), BF16)

    near, far, sends, feats, offset_map, cot, weights = run(
        pick_kernel,
        [
            halo, halo, struct((2, depth), jnp.int32), own,
            struct((offsets, 1, rows), jnp.int32), own, struct(w_second.shape, BF16),
        ],
        0,
        core,
        far_args=(
            send_rows[0, 0], features[0], jnp.transpose(neighbors, (1, 0, 2)), cotangent[0], w_second,
        ),
        scratch=[sem((5,))],
    )
    near, far = exchange(near, far)
    copied_grad, copied_pooled, columns, map_rows = run(
        copied_slots_kernel,
        [
            struct((copied, width), F32), struct((copied, offsets * width), BF16),
            struct((rows, 128), jnp.int32), struct((128, rows), jnp.int32),
        ],
        hot_flops // 3,
        core, offset_map, cot, weights,
    )
    gathered_input, pre, hidden, near, far, weights_wide = run(
        first_kernel,
        [wide, struct((rows, width), F32), own, pair, pair, struct((width, offsets * width), BF16)],
        hot_flops + conv_flops,
        core, far, near, columns, feats, sends, copied_grad,
        far_args=(w_first.reshape(stack), w_second),
        scratch=[pltpu.VMEM(pool.shape, BF16), pltpu.VMEM(stack, BF16), sem, sem((offsets,))],
    )
    near, far = exchange(near, far)
    own_grad, own_pooled = run(
        own_slots_kernel,
        [struct((rows, width), F32), wide],
        hot_flops,
        core, map_rows, cot, weights_wide, hidden,
    )
    pre_grad, given, hidden_pool = run(
        second_kernel,
        [own, struct(stack, BF16), pool],
        conv_flops,
        core, far, near, hidden, sends, own_grad, pre, gathered_input, own_pooled, copied_pooled,
    )

    extra = []

    def keep():
        kept, gathered = run(
            third_kernel,
            [struct(stack, F32), wide],
            conv_flops + hot_flops,
            core, gathered_input, pre_grad, hidden_pool, own_pooled, copied_pooled, columns,
        )
        extra.append(gathered)
        return kept

    def beside(part):
        return run(
            output_kernel,
            [own, struct(stack, BF16), struct(stack, BF16)],
            conv_flops,
            core, extra[0], feats, weights.reshape(stack),
            any_args=(part,),
            scratch=[sem((2,))],
            out_spaces=(pltpu.VMEM, pltpu.HBM, pltpu.HBM),
        )

    (output, grad_one, grad_two), other = summed(given, keep, beside)
    grad_one, grad_two = run(
        last_kernel,
        [struct(stack, BF16), struct(stack, BF16)],
        0,
        core,
        any_args=(other, grad_one, grad_two),
        scratch=[sem((2,))],
        out_spaces=(pltpu.HBM, pltpu.HBM),
        aliases={2: 0, 3: 1},
    )
    shape = (offsets, width, width)
    return (output[None], grad_one.reshape(shape), grad_two.reshape(shape))


def solution(mesh):
    fine = Mesh(mesh.devices.reshape(4, 8, 2, 8), SPACE + ("dp",))
    placed = (
        P("dp", SPACE, None),
        P("dp", SPACE, None),
        P(),
        P(),
        P("dp", None, SPACE),
        P("dp", SPACE, None, None),
    )
    return jax.shard_map(
        per_device,
        mesh=fine,
        in_specs=placed,
        out_specs=(P("dp", SPACE, None), P(), P()),
        check_vma=False,
    )
```

```python
import jax
import jax.numpy as jnp
from jax import lax
from jax.experimental import pallas as pl
from jax.experimental.pallas import tpu as pltpu
from jax.sharding import Mesh
from jax.sharding import PartitionSpec as P

SPACE = ("x", "y", "core")
PLANE = ("y", "dp")
BF16 = jnp.bfloat16
F32 = jnp.float32
VMEM_LIMIT = 24 * 1024 * 1024


def struct(shape, dtype):
    return jax.ShapeDtypeStruct(shape, dtype)


def run(kernel, outs, flops, *args, far_args=(), any_args=(), scratch=(), out_spaces=None, aliases=()):
    moved = sum(a.size * a.dtype.itemsize for a in (*args, *far_args, *outs))
    return pl.pallas_call(
        kernel,
        out_shape=outs,
        in_specs=[pl.BlockSpec(memory_space=pltpu.SMEM)]
        + [pl.BlockSpec(memory_space=pltpu.VMEM)] * (len(args) - 1)
        + [pl.BlockSpec(memory_space=pltpu.HBM)] * len(far_args)
        + [pl.BlockSpec(memory_space=pl.ANY)] * len(any_args),
        out_specs=[pl.BlockSpec(memory_space=space) for space in out_spaces or [pltpu.VMEM] * len(outs)],
        scratch_shapes=scratch,
        input_output_aliases=dict(aliases),
        compiler_params=pltpu.CompilerParams(vmem_limit_bytes=VMEM_LIMIT),
        cost_estimate=pl.CostEstimate(flops=flops, bytes_accessed=moved, transcendentals=0),
    )(*args, *(pltpu.with_memory_space_constraint(a, pltpu.HBM) for a in far_args), *any_args)


def dot(left, right, over=((1,), (0,))):
    return lax.dot_general(left, right, (over, ((), ())), preferred_element_type=F32)


ROWS_BOTH = ((0,), (0,))
COLS_BOTH = ((1,), (1,))


def send_lists(core, sends_ref):
    first = core == 0
    low, high = sends_ref[0:1, :], sends_ref[1:2, :]
    return jnp.where(first, high, low), jnp.where(first, low, high)


def placed_at(rows, listed):
    return (lax.broadcasted_iota(jnp.int32, (rows, listed.shape[1]), 0) == listed).astype(BF16)


def pick_kernel(
    core_ref, sends_hbm, feats_hbm, map_hbm, cot_hbm, weights_hbm,
    near_ref, far_ref, sends_ref, feats_ref, map_ref, cot_ref, weights_ref, sems,
):
    pairs = (
        (sends_hbm, sends_ref),
        (feats_hbm, feats_ref),
        (map_hbm, map_ref),
        (cot_hbm, cot_ref),
        (weights_hbm, weights_ref),
    )
    copies = [pltpu.make_async_copy(*pair, sems.at[i]) for i, pair in enumerate(pairs)]
    for copy in copies:
        copy.start()
    copies[0].wait()
    near, far = send_lists(core_ref[0], sends_ref)
    rows = feats_ref.shape[0]
    near, far = placed_at(rows, near), placed_at(rows, far)
    copies[1].wait()
    near_ref[...] = dot(near, feats_ref[...], ROWS_BOTH).astype(BF16)
    far_ref[...] = dot(far, feats_ref[...], ROWS_BOTH).astype(BF16)
    for copy in copies[2:]:
        copy.wait()


def pool_slots(rows_ref, cot_ref, first_slot, pooled_ref, width):
    slots, rows = pooled_ref.shape[0], rows_ref.shape[1]
    cot = cot_ref[...]
    slot = lax.broadcasted_iota(jnp.int32, (slots, rows), 0) + first_slot
    for k in range(pooled_ref.shape[1] // width):
        hot = (slot == rows_ref[k : k + 1, :]).astype(BF16)
        pooled_ref[:, k * width : (k + 1) * width] = dot(hot, cot).astype(BF16)


def copied_slots_kernel(core_ref, map_ref, cot_ref, weights_ref, grad_ref, pooled_ref, columns_ref, rows_ref):
    rows_ref[...] = jnp.zeros_like(rows_ref)
    offsets, width, _ = weights_ref.shape
    for k in range(offsets):
        rows_ref[k : k + 1, :] = map_ref[k]
    columns_ref[...] = rows_ref[...].T
    pool_slots(rows_ref, cot_ref, cot_ref.shape[0], pooled_ref, width)
    total = jnp.zeros(grad_ref.shape, F32)
    for k in range(offsets):
        total += dot(pooled_ref[:, k * width : (k + 1) * width], weights_ref[k], COLS_BOTH)
    grad_ref[...] = total


def own_slots_kernel(core_ref, rows_ref, cot_ref, weights_ref, hidden_ref, grad_ref, pooled_ref, weights_wide):
    width = cot_ref.shape[1]
    for k in range(weights_ref.shape[0]):
        weights_wide[:, k * width : (k + 1) * width] = weights_ref[k]
    pool_slots(rows_ref, cot_ref, 0, pooled_ref, width)
    grad_ref[...] = dot(pooled_ref[...], weights_wide[...], COLS_BOTH)


def fill_pool(core, pool, rows_ref, near, far):
    rows, depth = rows_ref.shape[0], near.shape[0]
    pool[:rows, :] = rows_ref[...]
    pool[pl.ds(pl.multiple_of(rows + depth * (1 - core), depth), depth), :] = near
    pool[pl.ds(pl.multiple_of(rows + depth * core, depth), depth), :] = far


def gather(columns_ref, pool_ref, gathered_ref):
    (rows, _), (slots, width) = columns_ref.shape, pool_ref.shape
    pool = pool_ref[...]
    slot = lax.broadcasted_iota(jnp.int32, (rows, slots), 1)
    for k in range(gathered_ref.shape[1] // width):
        hot = (slot == columns_ref[:, k : k + 1]).astype(BF16)
        gathered_ref[:, k * width : (k + 1) * width] = dot(hot, pool).astype(BF16)


def first_kernel(
    core_ref, far_ref, near_ref, columns_ref, feats_ref, sends_ref, grad_ref, weights_hbm,
    gathered_ref, pre_ref, hidden_ref, to_near_ref, to_far_ref, pool, weights, sem,
):
    copy = pltpu.make_async_copy(weights_hbm, weights, sem)
    copy.start()
    core = core_ref[0]
    rows, depth = feats_ref.shape[0], near_ref.shape[0]
    fill_pool(core, pool, feats_ref, near_ref[...], far_ref[...])
    gather(columns_ref, pool, gathered_ref)
    near, far = send_lists(core, sends_ref)
    before, after = grad_ref[:depth, :], grad_ref[depth:, :]
    to_near_ref[depth:, :] = jnp.where(core == 0, after, before).astype(BF16)
    to_far_ref[depth:, :] = jnp.where(core == 0, before, after).astype(BF16)
    copy.wait()
    pre = dot(gathered_ref[...], weights[...])
    pre_ref[...] = pre
    hidden = (pre * jax.nn.sigmoid(pre)).astype(BF16)
    hidden_ref[...] = hidden
    to_near_ref[:depth, :] = dot(placed_at(rows, near), hidden, ROWS_BOTH).astype(BF16)
    to_far_ref[:depth, :] = dot(placed_at(rows, far), hidden, ROWS_BOTH).astype(BF16)


def first_gradient(gathered_ref, pre_grad_ref, out_ref):
    out_ref[...] = dot(gathered_ref[...], pre_grad_ref[...], ROWS_BOTH).astype(out_ref.dtype)


def second_gradient(pool_ref, own_ref, copied_ref, out_ref):
    rows, wide = own_ref.shape
    width = pool_ref.shape[1]
    own, copied = pool_ref[:rows, :], pool_ref[rows:, :]
    for start in range(0, wide, 2 * width):
        stop = min(wide, start + 2 * width)
        part = dot(own, own_ref[:, start:stop], ROWS_BOTH) + dot(copied, copied_ref[:, start:stop], ROWS_BOTH)
        for column in range(start, stop, width):
            out_ref[column : column + width, :] = part[:, column - start : column - start + width].astype(
                out_ref.dtype
            )


def second_kernel(
    core_ref, far_ref, near_ref, hidden_ref, sends_ref, grad_ref, pre_ref, first_ref, own_ref, copied_ref,
    pre_grad_ref, given_ref, pool_ref,
):
    core = core_ref[0]
    rows, depth = hidden_ref.shape[0], near_ref.shape[0] // 2
    fill_pool(core, pool_ref, hidden_ref, near_ref[:depth, :], far_ref[:depth, :])
    near, far = send_lists(core, sends_ref)
    hidden_grad = (
        grad_ref[...]
        + dot(placed_at(rows, near), near_ref[depth:, :])
        + dot(placed_at(rows, far), far_ref[depth:, :])
    )
    pre = pre_ref[...]
    sigma = jax.nn.sigmoid(pre)
    pre_grad_ref[...] = (hidden_grad * sigma * (1.0 + pre * (1.0 - sigma))).astype(BF16)

    @pl.when(core == 0)
    def _():
        second_gradient(pool_ref, own_ref, copied_ref, given_ref)

    @pl.when(core != 0)
    def _():
        first_gradient(first_ref, pre_grad_ref, given_ref)


def third_kernel(core_ref, first_ref, pre_grad_ref, pool_ref, own_ref, copied_ref, kept_ref):
    core = core_ref[0]

    @pl.when(core == 0)
    def _():
        first_gradient(first_ref, pre_grad_ref, kept_ref)

    @pl.when(core != 0)
    def _():
        second_gradient(pool_ref, own_ref, copied_ref, kept_ref)


def output_kernel(
    core_ref, columns_ref, pool_ref, feats_ref, weights_ref, part_any,
    output_ref, one_hbm, two_hbm, gathered, sems,
):
    first = core_ref[0] == 0
    to_one = pltpu.make_async_copy(part_any, one_hbm, sems.at[0])
    to_two = pltpu.make_async_copy(part_any, two_hbm, sems.at[1])
    pl.when(first)(to_one.start)
    pl.when(jnp.logical_not(first))(to_two.start)
    gather(columns_ref, pool_ref, gathered)
    output_ref[...] = (dot(gathered[...], weights_ref[...]) + feats_ref[...].astype(F32)).astype(BF16)
    pl.when(first)(to_one.wait)
    pl.when(jnp.logical_not(first))(to_two.wait)


def last_kernel(core_ref, other_any, one_in, two_in, one_hbm, two_hbm, sems):
    first = core_ref[0] == 0
    to_one = pltpu.make_async_copy(other_any, one_hbm, sems.at[0])
    to_two = pltpu.make_async_copy(other_any, two_hbm, sems.at[1])
    pl.when(first)(to_two.start)
    pl.when(jnp.logical_not(first))(to_one.start)
    pl.when(first)(to_two.wait)
    pl.when(jnp.logical_not(first))(to_one.wait)


def exchange(near, far):
    size = lax.axis_size(SPACE)
    even = [(i, i ^ 1) for i in range(size)]
    odd = [(i, ((i - 1) ^ 1) + 1) for i in range(1, size - 1)]
    far = lax.ppermute(far, SPACE, odd)
    return lax.ppermute(near, SPACE, even), far


def scattered(part, axis):
    size = lax.axis_size(axis)
    pieces = lax.all_to_all(part.reshape(size, -1, part.shape[-1]), axis, 0, 0)
    return pieces.astype(F32).sum(0).astype(BF16)


def collected(part, axis):
    size = lax.axis_size(axis)
    pieces = lax.all_to_all(jnp.broadcast_to(part[None], (size,) + part.shape), axis, 0, 0)
    return pieces.reshape(-1, part.shape[-1])


def summed(given, keep, beside):
    swap = [(0, 1), (1, 0)]
    taken = lax.ppermute(given, "core", swap)
    part = (keep() + taken.astype(F32)).astype(BF16)
    part = scattered(part, "x")
    length = part.shape[0]
    peers = lax.axis_size(PLANE)
    block = 16 * -(-length // (16 * peers))
    part = jnp.pad(part, ((0, block * peers - length), (0, 0)))
    part = collected(scattered(part, PLANE), PLANE)[:length]
    part = collected(part, "x")
    other = lax.ppermute(part, "core", swap)
    return beside(part), other


def per_device(features, cotangent, w_first, w_second, neighbors, send_rows):
    core = lax.axis_index("core").astype(jnp.int32).reshape(1)
    _, rows, width = features.shape
    offsets, depth = neighbors.shape[1], send_rows.shape[-1]
    copied, slots = 2 * depth, rows + 2 * depth
    hot_flops = 2 * offsets * rows * slots * width
    conv_flops = 2 * offsets * rows * width * width
    own = struct((rows, width), BF16)
    halo = struct((depth, width), BF16)
    pair = struct((2 * depth, width), BF16)
    wide = struct((rows, offsets * width), BF16)
    stack = (offsets * width, width)
    sem = pltpu.SemaphoreType.DMA
    pool = struct((slots, width), BF16)

    near, far, sends, feats, offset_map, cot, weights = run(
        pick_kernel,
        [
            halo, halo, struct((2, depth), jnp.int32), own,
            struct((offsets, 1, rows), jnp.int32), own, struct(w_second.shape, BF16),
        ],
        0,
        core,
        far_args=(
            send_rows[0, 0], features[0], jnp.transpose(neighbors, (1, 0, 2)), cotangent[0], w_second,
        ),
        scratch=[sem((5,))],
    )
    near, far = exchange(near, far)
    copied_grad, copied_pooled, columns, map_rows = run(
        copied_slots_kernel,
        [
            struct((copied, width), F32), struct((copied, offsets * width), BF16),
            struct((rows, 128), jnp.int32), struct((128, rows), jnp.int32),
        ],
        hot_flops // 3,
        core, offset_map, cot, weights,
    )
    gathered_input, pre, hidden, near, far = run(
        first_kernel,
        [wide, struct((rows, width), F32), own, pair, pair],
        hot_flops + conv_flops,
        core, far, near, columns, feats, sends, copied_grad,
        far_args=(w_first.reshape(stack),),
        scratch=[pltpu.VMEM(pool.shape, BF16), pltpu.VMEM(stack, BF16), sem],
    )
    near, far = exchange(near, far)
    own_grad, own_pooled = run(
        own_slots_kernel,
        [struct((rows, width), F32), wide],
        hot_flops,
        core, map_rows, cot, weights, hidden,
        scratch=[pltpu.VMEM((width, offsets * width), BF16)],
    )
    pre_grad, given, hidden_pool = run(
        second_kernel,
        [own, struct(stack, BF16), pool],
        conv_flops,
        core, far, near, hidden, sends, own_grad, pre, gathered_input, own_pooled, copied_pooled,
    )

    def keep():
        return run(
            third_kernel,
            [struct(stack, F32)],
            conv_flops,
            core, gathered_input, pre_grad, hidden_pool, own_pooled, copied_pooled,
        )[0]

    def beside(part):
        return run(
            output_kernel,
            [own, struct(stack, BF16), struct(stack, BF16)],
            hot_flops + conv_flops,
            core, columns, hidden_pool, feats, weights.reshape(stack),
            any_args=(part,),
            scratch=[pltpu.VMEM(wide.shape, BF16), sem((2,))],
            out_spaces=(pltpu.VMEM, pltpu.HBM, pltpu.HBM),
        )

    (output, grad_one, grad_two), other = summed(given, keep, beside)
    grad_one, grad_two = run(
        last_kernel,
        [struct(stack, BF16), struct(stack, BF16)],
        0,
        core,
        any_args=(other, grad_one, grad_two),
        scratch=[sem((2,))],
        out_spaces=(pltpu.HBM, pltpu.HBM),
        aliases={2: 0, 3: 1},
    )
    shape = (offsets, width, width)
    return (output[None], grad_one.reshape(shape), grad_two.reshape(shape))


def solution(mesh):
    fine = Mesh(mesh.devices.reshape(4, 8, 2, 8), SPACE + ("dp",))
    placed = (
        P("dp", SPACE, None),
        P("dp", SPACE, None),
        P(),
        P(),
        P("dp", None, SPACE),
        P("dp", SPACE, None, None),
    )
    return jax.shard_map(
        per_device,
        mesh=fine,
        in_specs=placed,
        out_specs=(P("dp", SPACE, None), P(), P()),
        check_vma=False,
    )
```

```python
import jax
import jax.numpy as jnp
from jax import lax
from jax.experimental import pallas as pl
from jax.experimental.pallas import tpu as pltpu
from jax.sharding import Mesh
from jax.sharding import PartitionSpec as P

SPACE = ("x", "y", "core")
PLANE = ("y", "dp")
BF16 = jnp.bfloat16
F32 = jnp.float32
VMEM_LIMIT = 24 * 1024 * 1024


def struct(shape, dtype):
    return jax.ShapeDtypeStruct(shape, dtype)


def run(kernel, outs, flops, *args, far_args=(), any_args=(), scratch=(), out_spaces=None, aliases=()):
    moved = sum(a.size * a.dtype.itemsize for a in (*args, *far_args, *outs))
    return pl.pallas_call(
        kernel,
        out_shape=outs,
        in_specs=[pl.BlockSpec(memory_space=pltpu.SMEM)]
        + [pl.BlockSpec(memory_space=pltpu.VMEM)] * (len(args) - 1)
        + [pl.BlockSpec(memory_space=pltpu.HBM)] * len(far_args)
        + [pl.BlockSpec(memory_space=pl.ANY)] * len(any_args),
        out_specs=[pl.BlockSpec(memory_space=space) for space in out_spaces or [pltpu.VMEM] * len(outs)],
        scratch_shapes=scratch,
        input_output_aliases=dict(aliases),
        compiler_params=pltpu.CompilerParams(vmem_limit_bytes=VMEM_LIMIT),
        cost_estimate=pl.CostEstimate(flops=flops, bytes_accessed=moved, transcendentals=0),
    )(*args, *(pltpu.with_memory_space_constraint(a, pltpu.HBM) for a in far_args), *any_args)


def dot(left, right, over=((1,), (0,))):
    return lax.dot_general(left, right, (over, ((), ())), preferred_element_type=F32)


ROWS_BOTH = ((0,), (0,))
COLS_BOTH = ((1,), (1,))


def send_lists(core, sends_ref):
    first = core == 0
    low, high = sends_ref[0:1, :], sends_ref[1:2, :]
    return jnp.where(first, high, low), jnp.where(first, low, high)


def placed_at(rows, listed):
    return (lax.broadcasted_iota(jnp.int32, (rows, listed.shape[1]), 0) == listed).astype(BF16)


def pick_kernel(
    core_ref, sends_hbm, feats_hbm, map_hbm, cot_hbm, weights_hbm,
    near_ref, far_ref, sends_ref, feats_ref, map_ref, cot_ref, weights_ref, sems,
):
    pairs = (
        (sends_hbm, sends_ref),
        (feats_hbm, feats_ref),
        (map_hbm, map_ref),
        (cot_hbm, cot_ref),
        (weights_hbm, weights_ref),
    )
    copies = [pltpu.make_async_copy(*pair, sems.at[i]) for i, pair in enumerate(pairs)]
    for copy in copies:
        copy.start()
    copies[0].wait()
    near, far = send_lists(core_ref[0], sends_ref)
    rows = feats_ref.shape[0]
    near, far = placed_at(rows, near), placed_at(rows, far)
    copies[1].wait()
    near_ref[...] = dot(near, feats_ref[...], ROWS_BOTH).astype(BF16)
    far_ref[...] = dot(far, feats_ref[...], ROWS_BOTH).astype(BF16)
    for copy in copies[2:]:
        copy.wait()


def pool_slots(rows_ref, cot_ref, pooled_ref, width):
    slots, rows = pooled_ref.shape[0], rows_ref.shape[1]
    cot = cot_ref[...]
    slot = lax.broadcasted_iota(jnp.int32, (slots, rows), 0)
    for k in range(pooled_ref.shape[1] // width):
        hot = (slot == rows_ref[k : k + 1, :]).astype(BF16)
        pooled_ref[:, k * width : (k + 1) * width] = dot(hot, cot).astype(BF16)


def copied_slots_kernel(core_ref, map_ref, cot_ref, weights_ref, grad_ref, pooled_ref, columns_ref, rows_ref):
    rows_ref[...] = jnp.zeros_like(rows_ref)
    offsets, width, _ = weights_ref.shape
    for k in range(offsets):
        rows_ref[k : k + 1, :] = map_ref[k]
    columns_ref[...] = rows_ref[...].T
    cot = cot_ref[...]
    rows = cot.shape[0]
    slot = lax.broadcasted_iota(jnp.int32, (grad_ref.shape[0], rows), 0) + rows
    total = jnp.zeros(grad_ref.shape, F32)
    for k in range(offsets):
        pooled = dot((slot == rows_ref[k : k + 1, :]).astype(BF16), cot).astype(BF16)
        pooled_ref[:, k * width : (k + 1) * width] = pooled
        total += dot(pooled, weights_ref[k], COLS_BOTH)
    grad_ref[...] = total


def own_slots_kernel(core_ref, rows_ref, cot_ref, weights_ref, hidden_ref, grad_ref, pooled_ref, weights_wide):
    width = cot_ref.shape[1]
    for k in range(weights_ref.shape[0]):
        weights_wide[:, k * width : (k + 1) * width] = weights_ref[k]
    pool_slots(rows_ref, cot_ref, pooled_ref, width)
    grad_ref[...] = dot(pooled_ref[...], weights_wide[...], COLS_BOTH)


def fill_pool(core, pool, rows_ref, near, far):
    rows, depth = rows_ref.shape[0], near.shape[0]
    pool[:rows, :] = rows_ref[...]
    pool[pl.ds(pl.multiple_of(rows + depth * (1 - core), depth), depth), :] = near
    pool[pl.ds(pl.multiple_of(rows + depth * core, depth), depth), :] = far


def gather(columns_ref, pool_ref, gathered_ref, start=0):
    (rows, _), (slots, width) = columns_ref.shape, pool_ref.shape
    pool = pool_ref[...]
    slot = lax.broadcasted_iota(jnp.int32, (rows, slots), 1)
    for k in range(gathered_ref.shape[1] // width):
        hot = (slot == columns_ref[:, start + k : start + k + 1]).astype(BF16)
        gathered_ref[:, k * width : (k + 1) * width] = dot(hot, pool).astype(BF16)


def first_kernel(
    core_ref, far_ref, near_ref, columns_ref, feats_ref, sends_ref, grad_ref, weights_hbm,
    gathered_ref, pre_ref, hidden_ref, to_near_ref, to_far_ref, pool, weights, sem,
):
    copy = pltpu.make_async_copy(weights_hbm, weights, sem)
    copy.start()
    core = core_ref[0]
    rows, depth = feats_ref.shape[0], near_ref.shape[0]
    fill_pool(core, pool, feats_ref, near_ref[...], far_ref[...])
    gather(columns_ref, pool, gathered_ref)
    near, far = send_lists(core, sends_ref)
    before, after = grad_ref[:depth, :], grad_ref[depth:, :]
    to_near_ref[depth:, :] = jnp.where(core == 0, after, before).astype(BF16)
    to_far_ref[depth:, :] = jnp.where(core == 0, before, after).astype(BF16)
    copy.wait()
    pre = dot(gathered_ref[...], weights[...])
    pre_ref[...] = pre
    hidden = (pre * jax.nn.sigmoid(pre)).astype(BF16)
    hidden_ref[...] = hidden
    to_near_ref[:depth, :] = dot(placed_at(rows, near), hidden, ROWS_BOTH).astype(BF16)
    to_far_ref[:depth, :] = dot(placed_at(rows, far), hidden, ROWS_BOTH).astype(BF16)


def first_gradient(gathered_ref, pre_grad_ref, out_ref):
    out_ref[...] = dot(gathered_ref[...], pre_grad_ref[...], ROWS_BOTH).astype(out_ref.dtype)


def second_gradient(pool_ref, own_ref, copied_ref, out_ref):
    rows, wide = own_ref.shape
    width = pool_ref.shape[1]
    own, copied = pool_ref[:rows, :], pool_ref[rows:, :]
    for start in range(0, wide, 2 * width):
        stop = min(wide, start + 2 * width)
        part = dot(own, own_ref[:, start:stop], ROWS_BOTH) + dot(copied, copied_ref[:, start:stop], ROWS_BOTH)
        for column in range(start, stop, width):
            out_ref[column : column + width, :] = part[:, column - start : column - start + width].astype(
                out_ref.dtype
            )


def second_kernel(
    core_ref, far_ref, near_ref, hidden_ref, sends_ref, grad_ref, pre_ref, first_ref, own_ref, copied_ref,
    pre_grad_ref, given_ref, pool_ref,
):
    core = core_ref[0]
    rows, depth = hidden_ref.shape[0], near_ref.shape[0] // 2
    fill_pool(core, pool_ref, hidden_ref, near_ref[:depth, :], far_ref[:depth, :])
    near, far = send_lists(core, sends_ref)
    hidden_grad = (
        grad_ref[...]
        + dot(placed_at(rows, near), near_ref[depth:, :])
        + dot(placed_at(rows, far), far_ref[depth:, :])
    )
    pre = pre_ref[...]
    sigma = jax.nn.sigmoid(pre)
    pre_grad_ref[...] = (hidden_grad * sigma * (1.0 + pre * (1.0 - sigma))).astype(BF16)

    @pl.when(core == 0)
    def _():
        second_gradient(pool_ref, own_ref, copied_ref, given_ref)

    @pl.when(core != 0)
    def _():
        first_gradient(first_ref, pre_grad_ref, given_ref)


def third_kernel(
    core_ref, first_ref, pre_grad_ref, pool_ref, own_ref, copied_ref, columns_ref, feats_ref, weights_ref,
    kept_ref, partial_ref, gathered,
):
    core = core_ref[0]
    gather(columns_ref, pool_ref, gathered)
    partial_ref[...] = dot(gathered[...], weights_ref[: gathered.shape[1], :]) + feats_ref[...].astype(F32)

    @pl.when(core == 0)
    def _():
        first_gradient(first_ref, pre_grad_ref, kept_ref)

    @pl.when(core != 0)
    def _():
        second_gradient(pool_ref, own_ref, copied_ref, kept_ref)


def output_kernel(
    core_ref, columns_ref, pool_ref, partial_ref, weights_ref, part_any,
    output_ref, one_hbm, two_hbm, gathered, sems,
):
    first = core_ref[0] == 0
    to_one = pltpu.make_async_copy(part_any, one_hbm, sems.at[0])
    to_two = pltpu.make_async_copy(part_any, two_hbm, sems.at[1])
    pl.when(first)(to_one.start)
    pl.when(jnp.logical_not(first))(to_two.start)
    done = weights_ref.shape[0] - gathered.shape[1]
    gather(columns_ref, pool_ref, gathered, done // pool_ref.shape[1])
    output_ref[...] = (dot(gathered[...], weights_ref[done:, :]) + partial_ref[...]).astype(BF16)
    pl.when(first)(to_one.wait)
    pl.when(jnp.logical_not(first))(to_two.wait)


def last_kernel(core_ref, other_any, one_in, two_in, one_hbm, two_hbm, sems):
    first = core_ref[0] == 0
    to_one = pltpu.make_async_copy(other_any, one_hbm, sems.at[0])
    to_two = pltpu.make_async_copy(other_any, two_hbm, sems.at[1])
    pl.when(first)(to_two.start)
    pl.when(jnp.logical_not(first))(to_one.start)
    pl.when(first)(to_two.wait)
    pl.when(jnp.logical_not(first))(to_one.wait)


def exchange(near, far):
    size = lax.axis_size(SPACE)
    even = [(i, i ^ 1) for i in range(size)]
    odd = [(i, ((i - 1) ^ 1) + 1) for i in range(1, size - 1)]
    far = lax.ppermute(far, SPACE, odd)
    return lax.ppermute(near, SPACE, even), far


def scattered(part, axis):
    size = lax.axis_size(axis)
    pieces = lax.all_to_all(part.reshape(size, -1, part.shape[-1]), axis, 0, 0)
    return pieces.astype(F32).sum(0).astype(BF16)


def collected(part, axis):
    size = lax.axis_size(axis)
    pieces = lax.all_to_all(jnp.broadcast_to(part[None], (size,) + part.shape), axis, 0, 0)
    return pieces.reshape(-1, part.shape[-1])


def summed(given, keep, beside):
    swap = [(0, 1), (1, 0)]
    taken = lax.ppermute(given, "core", swap)
    part = (keep() + taken.astype(F32)).astype(BF16)
    part = scattered(part, "x")
    length = part.shape[0]
    peers = lax.axis_size(PLANE)
    block = 16 * -(-length // (16 * peers))
    part = jnp.pad(part, ((0, block * peers - length), (0, 0)))
    part = collected(scattered(part, PLANE), PLANE)[:length]
    part = collected(part, "x")
    other = lax.ppermute(part, "core", swap)
    return beside(part), other


def per_device(features, cotangent, w_first, w_second, neighbors, send_rows):
    core = lax.axis_index("core").astype(jnp.int32).reshape(1)
    _, rows, width = features.shape
    offsets, depth = neighbors.shape[1], send_rows.shape[-1]
    copied, slots = 2 * depth, rows + 2 * depth
    hot_flops = 2 * offsets * rows * slots * width
    conv_flops = 2 * offsets * rows * width * width
    own = struct((rows, width), BF16)
    halo = struct((depth, width), BF16)
    pair = struct((2 * depth, width), BF16)
    wide = struct((rows, offsets * width), BF16)
    stack = (offsets * width, width)
    sem = pltpu.SemaphoreType.DMA
    pool = struct((slots, width), BF16)

    near, far, sends, feats, offset_map, cot, weights = run(
        pick_kernel,
        [
            halo, halo, struct((2, depth), jnp.int32), own,
            struct((offsets, 1, rows), jnp.int32), own, struct(w_second.shape, BF16),
        ],
        0,
        core,
        far_args=(
            send_rows[0, 0], features[0], jnp.transpose(neighbors, (1, 0, 2)), cotangent[0], w_second,
        ),
        scratch=[sem((5,))],
    )
    near, far = exchange(near, far)
    copied_grad, copied_pooled, columns, map_rows = run(
        copied_slots_kernel,
        [
            struct((copied, width), F32), struct((copied, offsets * width), BF16),
            struct((rows, 128), jnp.int32), struct((128, rows), jnp.int32),
        ],
        hot_flops // 3,
        core, offset_map, cot, weights,
    )
    gathered_input, pre, hidden, near, far = run(
        first_kernel,
        [wide, struct((rows, width), F32), own, pair, pair],
        hot_flops + conv_flops,
        core, far, near, columns, feats, sends, copied_grad,
        far_args=(w_first.reshape(stack),),
        scratch=[pltpu.VMEM(pool.shape, BF16), pltpu.VMEM(stack, BF16), sem],
    )
    near, far = exchange(near, far)
    own_grad, own_pooled = run(
        own_slots_kernel,
        [struct((rows, width), F32), wide],
        hot_flops,
        core, map_rows, cot, weights, hidden,
        scratch=[pltpu.VMEM((width, offsets * width), BF16)],
    )
    pre_grad, given, hidden_pool = run(
        second_kernel,
        [own, struct(stack, BF16), pool],
        conv_flops,
        core, far, near, hidden, sends, own_grad, pre, gathered_input, own_pooled, copied_pooled,
    )

    early = offsets // 2
    partial = []

    def keep():
        kept, sums = run(
            third_kernel,
            [struct(stack, F32), struct((rows, width), F32)],
            conv_flops + (hot_flops + conv_flops) // 2,
            core, gathered_input, pre_grad, hidden_pool, own_pooled, copied_pooled, columns, feats,
            weights.reshape(stack),
            scratch=[pltpu.VMEM((rows, early * width), BF16)],
        )
        partial.append(sums)
        return kept

    def beside(part):
        return run(
            output_kernel,
            [own, struct(stack, BF16), struct(stack, BF16)],
            (hot_flops + conv_flops) // 2,
            core, columns, hidden_pool, partial[0], weights.reshape(stack),
            any_args=(part,),
            scratch=[pltpu.VMEM((rows, (offsets - early) * width), BF16), sem((2,))],
            out_spaces=(pltpu.VMEM, pltpu.HBM, pltpu.HBM),
        )

    (output, grad_one, grad_two), other = summed(given, keep, beside)
    grad_one, grad_two = run(
        last_kernel,
        [struct(stack, BF16), struct(stack, BF16)],
        0,
        core,
        any_args=(other, grad_one, grad_two),
        scratch=[sem((2,))],
        out_spaces=(pltpu.HBM, pltpu.HBM),
        aliases={2: 0, 3: 1},
    )
    shape = (offsets, width, width)
    return (output[None], grad_one.reshape(shape), grad_two.reshape(shape))


def solution(mesh):
    fine = Mesh(mesh.devices.reshape(4, 8, 2, 8), SPACE + ("dp",))
    placed = (
        P("dp", SPACE, None),
        P("dp", SPACE, None),
        P(),
        P(),
        P("dp", None, SPACE),
        P("dp", SPACE, None, None),
    )
    return jax.shard_map(
        per_device,
        mesh=fine,
        in_specs=placed,
        out_specs=(P("dp", SPACE, None), P(), P()),
        check_vma=False,
    )
```

```python
import jax
import jax.numpy as jnp
from jax import lax
from jax.experimental import pallas as pl
from jax.experimental.pallas import tpu as pltpu
from jax.sharding import Mesh
from jax.sharding import PartitionSpec as P

SPACE = ("x", "y", "core")
PLANE = ("dp", "y")
BF16 = jnp.bfloat16
F32 = jnp.float32
VMEM_LIMIT = 24 * 1024 * 1024


def struct(shape, dtype):
    return jax.ShapeDtypeStruct(shape, dtype)


def run(kernel, outs, flops, *args, far_args=(), any_args=(), scratch=(), out_spaces=None, aliases=()):
    moved = sum(a.size * a.dtype.itemsize for a in (*args, *far_args, *outs))
    return pl.pallas_call(
        kernel,
        out_shape=outs,
        in_specs=[pl.BlockSpec(memory_space=pltpu.SMEM)]
        + [pl.BlockSpec(memory_space=pltpu.VMEM)] * (len(args) - 1)
        + [pl.BlockSpec(memory_space=pltpu.HBM)] * len(far_args)
        + [pl.BlockSpec(memory_space=pl.ANY)] * len(any_args),
        out_specs=[pl.BlockSpec(memory_space=space) for space in out_spaces or [pltpu.VMEM] * len(outs)],
        scratch_shapes=scratch,
        input_output_aliases=dict(aliases),
        compiler_params=pltpu.CompilerParams(vmem_limit_bytes=VMEM_LIMIT),
        cost_estimate=pl.CostEstimate(flops=flops, bytes_accessed=moved, transcendentals=0),
    )(*args, *(pltpu.with_memory_space_constraint(a, pltpu.HBM) for a in far_args), *any_args)


def dot(left, right, over=((1,), (0,))):
    return lax.dot_general(left, right, (over, ((), ())), preferred_element_type=F32)


ROWS_BOTH = ((0,), (0,))
COLS_BOTH = ((1,), (1,))


def send_lists(core, sends_ref):
    first = core == 0
    low, high = sends_ref[0:1, :], sends_ref[1:2, :]
    return jnp.where(first, high, low), jnp.where(first, low, high)


def placed_at(rows, listed):
    return (lax.broadcasted_iota(jnp.int32, (rows, listed.shape[1]), 0) == listed).astype(BF16)


def pick_kernel(
    core_ref, sends_hbm, feats_hbm, map_hbm, cot_hbm, weights_hbm,
    near_ref, far_ref, sends_ref, feats_ref, map_ref, cot_ref, weights_ref, sems,
):
    pairs = (
        (sends_hbm, sends_ref),
        (feats_hbm, feats_ref),
        (map_hbm, map_ref),
        (cot_hbm, cot_ref),
        (weights_hbm, weights_ref),
    )
    copies = [pltpu.make_async_copy(*pair, sems.at[i]) for i, pair in enumerate(pairs)]
    for copy in copies:
        copy.start()
    copies[0].wait()
    near, far = send_lists(core_ref[0], sends_ref)
    rows = feats_ref.shape[0]
    near, far = placed_at(rows, near), placed_at(rows, far)
    copies[1].wait()
    near_ref[...] = dot(near, feats_ref[...], ROWS_BOTH).astype(BF16)
    far_ref[...] = dot(far, feats_ref[...], ROWS_BOTH).astype(BF16)
    for copy in copies[2:]:
        copy.wait()


def pool_slots(rows_ref, cot_ref, pooled_ref, width):
    slots, rows = pooled_ref.shape[0], rows_ref.shape[1]
    cot = cot_ref[...]
    slot = lax.broadcasted_iota(jnp.int32, (slots, rows), 0)
    for k in range(pooled_ref.shape[1] // width):
        hot = (slot == rows_ref[k : k + 1, :]).astype(BF16)
        pooled_ref[:, k * width : (k + 1) * width] = dot(hot, cot).astype(BF16)


def copied_slots_kernel(core_ref, map_ref, cot_ref, weights_ref, grad_ref, pooled_ref, columns_ref, rows_ref):
    rows_ref[...] = jnp.zeros_like(rows_ref)
    offsets, width, _ = weights_ref.shape
    for k in range(offsets):
        rows_ref[k : k + 1, :] = map_ref[k]
    columns_ref[...] = rows_ref[...].T
    cot = cot_ref[...]
    rows = cot.shape[0]
    slot = lax.broadcasted_iota(jnp.int32, (grad_ref.shape[0], rows), 0) + rows
    total = jnp.zeros(grad_ref.shape, F32)
    for k in range(offsets):
        pooled = dot((slot == rows_ref[k : k + 1, :]).astype(BF16), cot).astype(BF16)
        pooled_ref[:, k * width : (k + 1) * width] = pooled
        total += dot(pooled, weights_ref[k], COLS_BOTH)
    grad_ref[...] = total


def own_slots_kernel(core_ref, rows_ref, cot_ref, weights_ref, hidden_ref, grad_ref, pooled_ref, weights_wide):
    width = cot_ref.shape[1]
    for k in range(weights_ref.shape[0]):
        weights_wide[:, k * width : (k + 1) * width] = weights_ref[k]
    pool_slots(rows_ref, cot_ref, pooled_ref, width)
    grad_ref[...] = dot(pooled_ref[...], weights_wide[...], COLS_BOTH)


def fill_pool(core, pool, rows_ref, near, far):
    rows, depth = rows_ref.shape[0], near.shape[0]
    pool[:rows, :] = rows_ref[...]
    pool[pl.ds(pl.multiple_of(rows + depth * (1 - core), depth), depth), :] = near
    pool[pl.ds(pl.multiple_of(rows + depth * core, depth), depth), :] = far


def gather(columns_ref, pool_ref, gathered_ref, start=0):
    (rows, _), (slots, width) = columns_ref.shape, pool_ref.shape
    pool = pool_ref[...]
    slot = lax.broadcasted_iota(jnp.int32, (rows, slots), 1)
    for k in range(gathered_ref.shape[1] // width):
        hot = (slot == columns_ref[:, start + k : start + k + 1]).astype(BF16)
        gathered_ref[:, k * width : (k + 1) * width] = dot(hot, pool).astype(BF16)


def first_kernel(
    core_ref, far_ref, near_ref, columns_ref, feats_ref, sends_ref, grad_ref, weights_hbm,
    gathered_ref, pre_ref, hidden_ref, to_near_ref, to_far_ref, pool, weights, sem,
):
    copy = pltpu.make_async_copy(weights_hbm, weights, sem)
    copy.start()
    core = core_ref[0]
    rows, depth = feats_ref.shape[0], near_ref.shape[0]
    fill_pool(core, pool, feats_ref, near_ref[...], far_ref[...])
    gather(columns_ref, pool, gathered_ref)
    near, far = send_lists(core, sends_ref)
    before, after = grad_ref[:depth, :], grad_ref[depth:, :]
    to_near_ref[depth:, :] = jnp.where(core == 0, after, before).astype(BF16)
    to_far_ref[depth:, :] = jnp.where(core == 0, before, after).astype(BF16)
    copy.wait()
    pre = dot(gathered_ref[...], weights[...])
    pre_ref[...] = pre
    hidden = (pre * jax.nn.sigmoid(pre)).astype(BF16)
    hidden_ref[...] = hidden
    to_near_ref[:depth, :] = dot(placed_at(rows, near), hidden, ROWS_BOTH).astype(BF16)
    to_far_ref[:depth, :] = dot(placed_at(rows, far), hidden, ROWS_BOTH).astype(BF16)


def first_gradient(gathered_ref, pre_grad_ref, out_ref):
    out_ref[...] = dot(gathered_ref[...], pre_grad_ref[...], ROWS_BOTH).astype(out_ref.dtype)


def second_gradient(pool_ref, own_ref, copied_ref, out_ref):
    rows, wide = own_ref.shape
    width = pool_ref.shape[1]
    own, copied = pool_ref[:rows, :], pool_ref[rows:, :]
    for start in range(0, wide, 2 * width):
        stop = min(wide, start + 2 * width)
        part = dot(own, own_ref[:, start:stop], ROWS_BOTH) + dot(copied, copied_ref[:, start:stop], ROWS_BOTH)
        for column in range(start, stop, width):
            out_ref[column : column + width, :] = part[:, column - start : column - start + width].astype(
                out_ref.dtype
            )


def second_kernel(
    core_ref, far_ref, near_ref, hidden_ref, sends_ref, grad_ref, pre_ref, first_ref, own_ref, copied_ref,
    pre_grad_ref, given_ref, pool_ref,
):
    core = core_ref[0]
    rows, depth = hidden_ref.shape[0], near_ref.shape[0] // 2
    fill_pool(core, pool_ref, hidden_ref, near_ref[:depth, :], far_ref[:depth, :])
    near, far = send_lists(core, sends_ref)
    hidden_grad = (
        grad_ref[...]
        + dot(placed_at(rows, near), near_ref[depth:, :])
        + dot(placed_at(rows, far), far_ref[depth:, :])
    )
    pre = pre_ref[...]
    sigma = jax.nn.sigmoid(pre)
    pre_grad_ref[...] = (hidden_grad * sigma * (1.0 + pre * (1.0 - sigma))).astype(BF16)

    @pl.when(core == 0)
    def _():
        second_gradient(pool_ref, own_ref, copied_ref, given_ref)

    @pl.when(core != 0)
    def _():
        first_gradient(first_ref, pre_grad_ref, given_ref)


def third_kernel(
    core_ref, first_ref, pre_grad_ref, pool_ref, own_ref, copied_ref, columns_ref, feats_ref, weights_ref,
    kept_ref, partial_ref, gathered,
):
    core = core_ref[0]
    gather(columns_ref, pool_ref, gathered)
    partial_ref[...] = dot(gathered[...], weights_ref[: gathered.shape[1], :]) + feats_ref[...].astype(F32)

    @pl.when(core == 0)
    def _():
        first_gradient(first_ref, pre_grad_ref, kept_ref)

    @pl.when(core != 0)
    def _():
        second_gradient(pool_ref, own_ref, copied_ref, kept_ref)


def output_kernel(
    core_ref, columns_ref, pool_ref, partial_ref, weights_ref, part_any,
    output_ref, one_hbm, two_hbm, gathered, sems,
):
    first = core_ref[0] == 0
    to_one = pltpu.make_async_copy(part_any, one_hbm, sems.at[0])
    to_two = pltpu.make_async_copy(part_any, two_hbm, sems.at[1])
    pl.when(first)(to_one.start)
    pl.when(jnp.logical_not(first))(to_two.start)
    done = weights_ref.shape[0] - gathered.shape[1]
    gather(columns_ref, pool_ref, gathered, done // pool_ref.shape[1])
    output_ref[...] = (dot(gathered[...], weights_ref[done:, :]) + partial_ref[...]).astype(BF16)
    pl.when(first)(to_one.wait)
    pl.when(jnp.logical_not(first))(to_two.wait)


def last_kernel(core_ref, other_any, one_in, two_in, one_hbm, two_hbm, sems):
    first = core_ref[0] == 0
    to_one = pltpu.make_async_copy(other_any, one_hbm, sems.at[0])
    to_two = pltpu.make_async_copy(other_any, two_hbm, sems.at[1])
    pl.when(first)(to_two.start)
    pl.when(jnp.logical_not(first))(to_one.start)
    pl.when(first)(to_two.wait)
    pl.when(jnp.logical_not(first))(to_one.wait)


def exchange(near, far):
    size = lax.axis_size(SPACE)
    even = [(i, i ^ 1) for i in range(size)]
    odd = [(i, ((i - 1) ^ 1) + 1) for i in range(1, size - 1)]
    far = lax.ppermute(far, SPACE, odd)
    return lax.ppermute(near, SPACE, even), far


def scattered(part, axis):
    size = lax.axis_size(axis)
    pieces = lax.all_to_all(part.reshape(size, -1, part.shape[-1]), axis, 0, 0)
    return pieces.astype(F32).sum(0).astype(BF16)


def collected(part, axis):
    size = lax.axis_size(axis)
    pieces = lax.all_to_all(jnp.broadcast_to(part[None], (size,) + part.shape), axis, 0, 0)
    return pieces.reshape(-1, part.shape[-1])


def summed(given, keep, beside):
    swap = [(0, 1), (1, 0)]
    taken = lax.ppermute(given, "core", swap)
    part = (keep() + taken.astype(F32)).astype(BF16)
    part = scattered(part, "x")
    length = part.shape[0]
    peers = lax.axis_size(PLANE)
    block = 16 * -(-length // (16 * peers))
    part = jnp.pad(part, ((0, block * peers - length), (0, 0)))
    part = collected(scattered(part, PLANE), PLANE)[:length]
    part = collected(part, "x")
    other = lax.ppermute(part, "core", swap)
    return beside(part), other


def per_device(features, cotangent, w_first, w_second, neighbors, send_rows):
    core = lax.axis_index("core").astype(jnp.int32).reshape(1)
    _, rows, width = features.shape
    offsets, depth = neighbors.shape[1], send_rows.shape[-1]
    copied, slots = 2 * depth, rows + 2 * depth
    hot_flops = 2 * offsets * rows * slots * width
    conv_flops = 2 * offsets * rows * width * width
    own = struct((rows, width), BF16)
    halo = struct((depth, width), BF16)
    pair = struct((2 * depth, width), BF16)
    wide = struct((rows, offsets * width), BF16)
    stack = (offsets * width, width)
    sem = pltpu.SemaphoreType.DMA
    pool = struct((slots, width), BF16)

    near, far, sends, feats, offset_map, cot, weights = run(
        pick_kernel,
        [
            halo, halo, struct((2, depth), jnp.int32), own,
            struct((offsets, 1, rows), jnp.int32), own, struct(w_second.shape, BF16),
        ],
        0,
        core,
        far_args=(
            send_rows[0, 0], features[0], jnp.transpose(neighbors, (1, 0, 2)), cotangent[0], w_second,
        ),
        scratch=[sem((5,))],
    )
    near, far = exchange(near, far)
    copied_grad, copied_pooled, columns, map_rows = run(
        copied_slots_kernel,
        [
            struct((copied, width), F32), struct((copied, offsets * width), BF16),
            struct((rows, 128), jnp.int32), struct((128, rows), jnp.int32),
        ],
        hot_flops // 3,
        core, offset_map, cot, weights,
    )
    gathered_input, pre, hidden, near, far = run(
        first_kernel,
        [wide, struct((rows, width), F32), own, pair, pair],
        hot_flops + conv_flops,
        core, far, near, columns, feats, sends, copied_grad,
        far_args=(w_first.reshape(stack),),
        scratch=[pltpu.VMEM(pool.shape, BF16), pltpu.VMEM(stack, BF16), sem],
    )
    near, far = exchange(near, far)
    own_grad, own_pooled = run(
        own_slots_kernel,
        [struct((rows, width), F32), wide],
        hot_flops,
        core, map_rows, cot, weights, hidden,
        scratch=[pltpu.VMEM((width, offsets * width), BF16)],
    )
    pre_grad, given, hidden_pool = run(
        second_kernel,
        [own, struct(stack, BF16), pool],
        conv_flops,
        core, far, near, hidden, sends, own_grad, pre, gathered_input, own_pooled, copied_pooled,
    )

    early = offsets // 2
    partial = []

    def keep():
        kept, sums = run(
            third_kernel,
            [struct(stack, F32), struct((rows, width), F32)],
            conv_flops + (hot_flops + conv_flops) // 2,
            core, gathered_input, pre_grad, hidden_pool, own_pooled, copied_pooled, columns, feats,
            weights.reshape(stack),
            scratch=[pltpu.VMEM((rows, early * width), BF16)],
        )
        partial.append(sums)
        return kept

    def beside(part):
        return run(
            output_kernel,
            [own, struct(stack, BF16), struct(stack, BF16)],
            (hot_flops + conv_flops) // 2,
            core, columns, hidden_pool, partial[0], weights.reshape(stack),
            any_args=(part,),
            scratch=[pltpu.VMEM((rows, (offsets - early) * width), BF16), sem((2,))],
            out_spaces=(pltpu.VMEM, pltpu.HBM, pltpu.HBM),
        )

    (output, grad_one, grad_two), other = summed(given, keep, beside)
    grad_one, grad_two = run(
        last_kernel,
        [struct(stack, BF16), struct(stack, BF16)],
        0,
        core,
        any_args=(other, grad_one, grad_two),
        scratch=[sem((2,))],
        out_spaces=(pltpu.HBM, pltpu.HBM),
        aliases={2: 0, 3: 1},
    )
    shape = (offsets, width, width)
    return (output[None], grad_one.reshape(shape), grad_two.reshape(shape))


def solution(mesh):
    fine = Mesh(mesh.devices.reshape(4, 8, 2, 8), SPACE + ("dp",))
    placed = (
        P("dp", SPACE, None),
        P("dp", SPACE, None),
        P(),
        P(),
        P("dp", None, SPACE),
        P("dp", SPACE, None, None),
    )
    return jax.shard_map(
        per_device,
        mesh=fine,
        in_specs=placed,
        out_specs=(P("dp", SPACE, None), P(), P()),
        check_vma=False,
    )
```

```python
import jax
import jax.numpy as jnp
from jax import lax
from jax.experimental import pallas as pl
from jax.experimental.pallas import tpu as pltpu
from jax.sharding import Mesh
from jax.sharding import PartitionSpec as P

SPACE = ("x", "y", "core")
PLANE = ("y", "dp")
BF16 = jnp.bfloat16
F32 = jnp.float32
VMEM_LIMIT = 24 * 1024 * 1024


def struct(shape, dtype):
    return jax.ShapeDtypeStruct(shape, dtype)


def run(kernel, outs, flops, *args, far_args=(), any_args=(), scratch=(), out_spaces=None, aliases=()):
    moved = sum(a.size * a.dtype.itemsize for a in (*args, *far_args, *outs))
    return pl.pallas_call(
        kernel,
        out_shape=outs,
        in_specs=[pl.BlockSpec(memory_space=pltpu.SMEM)]
        + [pl.BlockSpec(memory_space=pltpu.VMEM)] * (len(args) - 1)
        + [pl.BlockSpec(memory_space=pltpu.HBM)] * len(far_args)
        + [pl.BlockSpec(memory_space=pl.ANY)] * len(any_args),
        out_specs=[pl.BlockSpec(memory_space=space) for space in out_spaces or [pltpu.VMEM] * len(outs)],
        scratch_shapes=scratch,
        input_output_aliases=dict(aliases),
        compiler_params=pltpu.CompilerParams(vmem_limit_bytes=VMEM_LIMIT),
        cost_estimate=pl.CostEstimate(flops=flops, bytes_accessed=moved, transcendentals=0),
    )(*args, *(pltpu.with_memory_space_constraint(a, pltpu.HBM) for a in far_args), *any_args)


def dot(left, right, over=((1,), (0,))):
    return lax.dot_general(left, right, (over, ((), ())), preferred_element_type=F32)


ROWS_BOTH = ((0,), (0,))
COLS_BOTH = ((1,), (1,))


def send_lists(core, sends_ref):
    first = core == 0
    low, high = sends_ref[0:1, :], sends_ref[1:2, :]
    return jnp.where(first, high, low), jnp.where(first, low, high)


def placed_at(rows, listed):
    return (lax.broadcasted_iota(jnp.int32, (rows, listed.shape[1]), 0) == listed).astype(BF16)


def pick_kernel(
    core_ref, sends_hbm, feats_hbm, map_hbm, cot_hbm, weights_hbm,
    near_ref, far_ref, sends_ref, feats_ref, cot_ref, weights_ref, columns_ref, rows_ref, map_ref, sems,
):
    pairs = (
        (sends_hbm, sends_ref),
        (feats_hbm, feats_ref),
        (map_hbm, map_ref),
        (cot_hbm, cot_ref),
        (weights_hbm, weights_ref),
    )
    copies = [pltpu.make_async_copy(*pair, sems.at[i]) for i, pair in enumerate(pairs)]
    for copy in copies:
        copy.start()
    copies[0].wait()
    near, far = send_lists(core_ref[0], sends_ref)
    rows = feats_ref.shape[0]
    near, far = placed_at(rows, near), placed_at(rows, far)
    copies[1].wait()
    near_ref[...] = dot(near, feats_ref[...], ROWS_BOTH).astype(BF16)
    far_ref[...] = dot(far, feats_ref[...], ROWS_BOTH).astype(BF16)
    copies[2].wait()
    rows_ref[...] = jnp.zeros_like(rows_ref)
    for k in range(map_ref.shape[0]):
        rows_ref[k : k + 1, :] = map_ref[k]
    columns_ref[...] = rows_ref[...].T
    for copy in copies[3:]:
        copy.wait()


def pool_slots(rows_ref, cot_ref, pooled_ref, width):
    slots, rows = pooled_ref.shape[0], rows_ref.shape[1]
    cot = cot_ref[...]
    slot = lax.broadcasted_iota(jnp.int32, (slots, rows), 0)
    for k in range(pooled_ref.shape[1] // width):
        hot = (slot == rows_ref[k : k + 1, :]).astype(BF16)
        pooled_ref[:, k * width : (k + 1) * width] = dot(hot, cot).astype(BF16)


def copied_slots_kernel(core_ref, rows_ref, cot_ref, weights_ref, grad_ref, pooled_ref):
    offsets, width, _ = weights_ref.shape
    cot = cot_ref[...]
    rows = cot.shape[0]
    slot = lax.broadcasted_iota(jnp.int32, (grad_ref.shape[0], rows), 0) + rows
    total = jnp.zeros(grad_ref.shape, F32)
    for k in range(offsets):
        pooled = dot((slot == rows_ref[k : k + 1, :]).astype(BF16), cot).astype(BF16)
        pooled_ref[:, k * width : (k + 1) * width] = pooled
        total += dot(pooled, weights_ref[k], COLS_BOTH)
    grad_ref[...] = total


def own_slots_kernel(core_ref, rows_ref, cot_ref, weights_ref, hidden_ref, grad_ref, pooled_ref, weights_wide):
    width = cot_ref.shape[1]
    for k in range(weights_ref.shape[0]):
        weights_wide[:, k * width : (k + 1) * width] = weights_ref[k]
    pool_slots(rows_ref, cot_ref, pooled_ref, width)
    grad_ref[...] = dot(pooled_ref[...], weights_wide[...], COLS_BOTH)


def fill_pool(core, pool, rows_ref, near, far):
    rows, depth = rows_ref.shape[0], near.shape[0]
    pool[:rows, :] = rows_ref[...]
    pool[pl.ds(pl.multiple_of(rows + depth * (1 - core), depth), depth), :] = near
    pool[pl.ds(pl.multiple_of(rows + depth * core, depth), depth), :] = far


def gather(columns_ref, pool_ref, gathered_ref, start=0):
    (rows, _), (slots, width) = columns_ref.shape, pool_ref.shape
    pool = pool_ref[...]
    slot = lax.broadcasted_iota(jnp.int32, (rows, slots), 1)
    for k in range(gathered_ref.shape[1] // width):
        hot = (slot == columns_ref[:, start + k : start + k + 1]).astype(BF16)
        gathered_ref[:, k * width : (k + 1) * width] = dot(hot, pool).astype(BF16)


def first_kernel(
    core_ref, far_ref, near_ref, columns_ref, feats_ref, sends_ref, grad_ref, weights_hbm,
    gathered_ref, pre_ref, hidden_ref, to_near_ref, to_far_ref, pool, weights, sem,
):
    copy = pltpu.make_async_copy(weights_hbm, weights, sem)
    copy.start()
    core = core_ref[0]
    rows, depth = feats_ref.shape[0], near_ref.shape[0]
    fill_pool(core, pool, feats_ref, near_ref[...], far_ref[...])
    gather(columns_ref, pool, gathered_ref)
    near, far = send_lists(core, sends_ref)
    before, after = grad_ref[:depth, :], grad_ref[depth:, :]
    to_near_ref[depth:, :] = jnp.where(core == 0, after, before).astype(BF16)
    to_far_ref[depth:, :] = jnp.where(core == 0, before, after).astype(BF16)
    copy.wait()
    pre = dot(gathered_ref[...], weights[...])
    pre_ref[...] = pre
    hidden = (pre * jax.nn.sigmoid(pre)).astype(BF16)
    hidden_ref[...] = hidden
    to_near_ref[:depth, :] = dot(placed_at(rows, near), hidden, ROWS_BOTH).astype(BF16)
    to_far_ref[:depth, :] = dot(placed_at(rows, far), hidden, ROWS_BOTH).astype(BF16)


def first_gradient(gathered_ref, pre_grad_ref, out_ref):
    out_ref[...] = dot(gathered_ref[...], pre_grad_ref[...], ROWS_BOTH).astype(out_ref.dtype)


def second_gradient(pool_ref, own_ref, copied_ref, out_ref):
    rows, wide = own_ref.shape
    width = pool_ref.shape[1]
    own, copied = pool_ref[:rows, :], pool_ref[rows:, :]
    for start in range(0, wide, 2 * width):
        stop = min(wide, start + 2 * width)
        part = dot(own, own_ref[:, start:stop], ROWS_BOTH) + dot(copied, copied_ref[:, start:stop], ROWS_BOTH)
        for column in range(start, stop, width):
            out_ref[column : column + width, :] = part[:, column - start : column - start + width].astype(
                out_ref.dtype
            )


def second_kernel(
    core_ref, far_ref, near_ref, hidden_ref, sends_ref, grad_ref, pre_ref, first_ref, own_ref, copied_ref,
    pre_grad_ref, given_ref, pool_ref,
):
    core = core_ref[0]
    rows, depth = hidden_ref.shape[0], near_ref.shape[0] // 2
    fill_pool(core, pool_ref, hidden_ref, near_ref[:depth, :], far_ref[:depth, :])
    near, far = send_lists(core, sends_ref)
    hidden_grad = (
        grad_ref[...]
        + dot(placed_at(rows, near), near_ref[depth:, :])
        + dot(placed_at(rows, far), far_ref[depth:, :])
    )
    pre = pre_ref[...]
    sigma = jax.nn.sigmoid(pre)
    pre_grad_ref[...] = (hidden_grad * sigma * (1.0 + pre * (1.0 - sigma))).astype(BF16)

    @pl.when(core == 0)
    def _():
        second_gradient(pool_ref, own_ref, copied_ref, given_ref)

    @pl.when(core != 0)
    def _():
        first_gradient(first_ref, pre_grad_ref, given_ref)


def third_kernel(
    core_ref, first_ref, pre_grad_ref, pool_ref, own_ref, copied_ref, columns_ref, feats_ref, weights_ref,
    kept_ref, partial_ref, gathered,
):
    core = core_ref[0]
    gather(columns_ref, pool_ref, gathered)
    partial_ref[...] = dot(gathered[...], weights_ref[: gathered.shape[1], :]) + feats_ref[...].astype(F32)

    @pl.when(core == 0)
    def _():
        first_gradient(first_ref, pre_grad_ref, kept_ref)

    @pl.when(core != 0)
    def _():
        second_gradient(pool_ref, own_ref, copied_ref, kept_ref)


def output_kernel(
    core_ref, columns_ref, pool_ref, partial_ref, weights_ref, part_any,
    output_ref, one_hbm, two_hbm, gathered, sems,
):
    first = core_ref[0] == 0
    to_one = pltpu.make_async_copy(part_any, one_hbm, sems.at[0])
    to_two = pltpu.make_async_copy(part_any, two_hbm, sems.at[1])
    pl.when(first)(to_one.start)
    pl.when(jnp.logical_not(first))(to_two.start)
    done = weights_ref.shape[0] - gathered.shape[1]
    gather(columns_ref, pool_ref, gathered, done // pool_ref.shape[1])
    output_ref[...] = (dot(gathered[...], weights_ref[done:, :]) + partial_ref[...]).astype(BF16)
    pl.when(first)(to_one.wait)
    pl.when(jnp.logical_not(first))(to_two.wait)


def last_kernel(core_ref, other_any, one_in, two_in, one_hbm, two_hbm, sems):
    first = core_ref[0] == 0
    to_one = pltpu.make_async_copy(other_any, one_hbm, sems.at[0])
    to_two = pltpu.make_async_copy(other_any, two_hbm, sems.at[1])
    pl.when(first)(to_two.start)
    pl.when(jnp.logical_not(first))(to_one.start)
    pl.when(first)(to_two.wait)
    pl.when(jnp.logical_not(first))(to_one.wait)


def exchange(near, far):
    size = lax.axis_size(SPACE)
    even = [(i, i ^ 1) for i in range(size)]
    odd = [(i, ((i - 1) ^ 1) + 1) for i in range(1, size - 1)]
    far = lax.ppermute(far, SPACE, odd)
    return lax.ppermute(near, SPACE, even), far


def scattered(part, axis):
    size = lax.axis_size(axis)
    pieces = lax.all_to_all(part.reshape(size, -1, part.shape[-1]), axis, 0, 0)
    return pieces.astype(F32).sum(0).astype(BF16)


def collected(part, axis):
    size = lax.axis_size(axis)
    pieces = lax.all_to_all(jnp.broadcast_to(part[None], (size,) + part.shape), axis, 0, 0)
    return pieces.reshape(-1, part.shape[-1])


def summed(given, keep, beside):
    swap = [(0, 1), (1, 0)]
    taken = lax.ppermute(given, "core", swap)
    part = (keep() + taken.astype(F32)).astype(BF16)
    part = scattered(part, "x")
    length = part.shape[0]
    peers = lax.axis_size(PLANE)
    block = 16 * -(-length // (16 * peers))
    part = jnp.pad(part, ((0, block * peers - length), (0, 0)))
    part = collected(scattered(part, PLANE), PLANE)[:length]
    part = collected(part, "x")
    other = lax.ppermute(part, "core", swap)
    return beside(part), other


def per_device(features, cotangent, w_first, w_second, neighbors, send_rows):
    core = lax.axis_index("core").astype(jnp.int32).reshape(1)
    _, rows, width = features.shape
    offsets, depth = neighbors.shape[1], send_rows.shape[-1]
    copied, slots = 2 * depth, rows + 2 * depth
    hot_flops = 2 * offsets * rows * slots * width
    conv_flops = 2 * offsets * rows * width * width
    own = struct((rows, width), BF16)
    halo = struct((depth, width), BF16)
    pair = struct((2 * depth, width), BF16)
    wide = struct((rows, offsets * width), BF16)
    stack = (offsets * width, width)
    sem = pltpu.SemaphoreType.DMA
    pool = struct((slots, width), BF16)

    near, far, sends, feats, cot, weights, columns, map_rows = run(
        pick_kernel,
        [
            halo, halo, struct((2, depth), jnp.int32), own, own, struct(w_second.shape, BF16),
            struct((rows, 128), jnp.int32), struct((128, rows), jnp.int32),
        ],
        0,
        core,
        far_args=(
            send_rows[0, 0], features[0], jnp.transpose(neighbors, (1, 0, 2)), cotangent[0], w_second,
        ),
        scratch=[pltpu.VMEM((offsets, 1, rows), jnp.int32), sem((5,))],
    )
    near, far = exchange(near, far)
    copied_grad, copied_pooled = run(
        copied_slots_kernel,
        [struct((copied, width), F32), struct((copied, offsets * width), BF16)],
        hot_flops // 3,
        core, map_rows, cot, weights,
    )
    gathered_input, pre, hidden, near, far = run(
        first_kernel,
        [wide, struct((rows, width), F32), own, pair, pair],
        hot_flops + conv_flops,
        core, far, near, columns, feats, sends, copied_grad,
        far_args=(w_first.reshape(stack),),
        scratch=[pltpu.VMEM(pool.shape, BF16), pltpu.VMEM(stack, BF16), sem],
    )
    near, far = exchange(near, far)
    own_grad, own_pooled = run(
        own_slots_kernel,
        [struct((rows, width), F32), wide],
        hot_flops,
        core, map_rows, cot, weights, hidden,
        scratch=[pltpu.VMEM((width, offsets * width), BF16)],
    )
    pre_grad, given, hidden_pool = run(
        second_kernel,
        [own, struct(stack, BF16), pool],
        conv_flops,
        core, far, near, hidden, sends, own_grad, pre, gathered_input, own_pooled, copied_pooled,
    )

    early = offsets // 2
    partial = []

    def keep():
        kept, sums = run(
            third_kernel,
            [struct(stack, F32), struct((rows, width), F32)],
            conv_flops + (hot_flops + conv_flops) // 2,
            core, gathered_input, pre_grad, hidden_pool, own_pooled, copied_pooled, columns, feats,
            weights.reshape(stack),
            scratch=[pltpu.VMEM((rows, early * width), BF16)],
        )
        partial.append(sums)
        return kept

    def beside(part):
        return run(
            output_kernel,
            [own, struct(stack, BF16), struct(stack, BF16)],
            (hot_flops + conv_flops) // 2,
            core, columns, hidden_pool, partial[0], weights.reshape(stack),
            any_args=(part,),
            scratch=[pltpu.VMEM((rows, (offsets - early) * width), BF16), sem((2,))],
            out_spaces=(pltpu.VMEM, pltpu.HBM, pltpu.HBM),
        )

    (output, grad_one, grad_two), other = summed(given, keep, beside)
    grad_one, grad_two = run(
        last_kernel,
        [struct(stack, BF16), struct(stack, BF16)],
        0,
        core,
        any_args=(other, grad_one, grad_two),
        scratch=[sem((2,))],
        out_spaces=(pltpu.HBM, pltpu.HBM),
        aliases={2: 0, 3: 1},
    )
    shape = (offsets, width, width)
    return (output[None], grad_one.reshape(shape), grad_two.reshape(shape))


def solution(mesh):
    fine = Mesh(mesh.devices.reshape(4, 8, 2, 8), SPACE + ("dp",))
    placed = (
        P("dp", SPACE, None),
        P("dp", SPACE, None),
        P(),
        P(),
        P("dp", None, SPACE),
        P("dp", SPACE, None, None),
    )
    return jax.shard_map(
        per_device,
        mesh=fine,
        in_specs=placed,
        out_specs=(P("dp", SPACE, None), P(), P()),
        check_vma=False,
    )
```
